256 devices in a mesh: head: 16 (over z, x_lo), blk: 16 (over x_hi, y, core).
Axes of the slice: x: 4 (x_hi: 2, x_lo: 2; x = x_hi * 2 + x_lo), y: 4, z: 8, core: 2. Of those that a mesh axis runs over, the one named last changes fastest.
Arguments:
- queries: bfloat16 [2, 16384, 2048], P(None, ('head', 'blk')), may hold values from -320 to 320
- key_codes: bfloat16 [2, 16384, 2048], P(None, ('head', 'blk')), may hold values from -6 to 6
- key_scales: bfloat16 [2, 16384, 16], P(None, ('head', 'blk')), may hold values from 0.5 to 2
- value_codes: bfloat16 [2, 16384, 2048], P(None, ('head', 'blk')), may hold values from -6 to 6
- value_scales: bfloat16 [2, 16384, 16], P(None, ('head', 'blk')), may hold values from 0.5 to 2
- doc_lengths: int32 [2, 8], replicated, may hold values from 1 to 8192, 16384 in all within a row
Outputs:
- attended: bfloat16 [2, 16384, 2048], P(None, ('head', 'blk'))
The draws below stay inside these ranges and needn't reach their ends.
All inputs are finite; a program needn't handle non-finite values.
Results may differ from the reference program's by a relative error of at most 0.0055.
The reference program's roundings to bfloat16 on the way count: a program that leaves them out, or rounds other values in their place, can miss the bound.
Values may be sent and summed in bfloat16 or wider, within the bound.
A program may use at most 128 MiB of HBM per device.

```python
import math
import jax
import jax.numpy as jnp
import numpy as np
from jax import lax

H = 16
DH = 128
D = 2048
SEQS = 2
NDOC = 8
SEQ_LEN = 16384


def draw_queries(key, part):
    key = jax.random.fold_in(key, 11)
    noise_key = jax.random.fold_in(key, 0)
    base = jnp.clip(jax.random.normal(noise_key, (SEQS, SEQ_LEN, D), jnp.float32), -4.0, 4.0)
    return base.astype(jnp.bfloat16)


def levels(own_key, dims, pieces, smallest, largest):
    loudness, own = 1.0, jax.random.fold_in(own_key, 6)
    for dim, blocks in pieces:
        heights = jnp.exp(jax.random.uniform(jax.random.fold_in(own, dim), (blocks,), jnp.float32, smallest / len(pieces), largest / len(pieces)))
        loudness = loudness * jnp.repeat(heights, dims[dim] // blocks).reshape([-1 if axis == dim else 1 for axis in range(len(dims))])
    return loudness


def profile(number_of, total, bound, slope):
    loads = [(1 << 20) // math.isqrt(grade ** slope) + 1 for grade in range(2, number_of + 1)]
    rest, given = total - bound - (number_of - 1), [1] * (number_of - 1)
    while rest > 0:
        free = [i for i in range(number_of - 1) if given[i] < bound]
        whole, remaining = sum([loads[i] for i in free]), rest
        for i in free:
            extra = min(bound - given[i], max(1, remaining * loads[i] // whole), rest)
            given[i] = given[i] + extra
            rest = rest - extra
    return np.array([bound] + given)


def ragged(rng, count, total, bound, skew):
    if count == 2:
        one = jax.random.randint(rng, (), max(1, total - bound), min(bound, total - 1) + 1)
        return jnp.stack([one, total - one])
    lengths = jnp.asarray(profile(count, total, bound, skew), jnp.int32)
    pairs = (count - 1) // 2
    source_of, sink = lengths[1:1 + 2 * pairs:2], lengths[2:2 + 2 * pairs:2]
    margin = jnp.minimum(source_of - 1, bound - sink)
    passed = jax.random.randint(jax.random.fold_in(rng, 1), (pairs,), 0, 1 << 20) % (margin + 1)
    lengths = lengths.at[1:1 + 2 * pairs:2].set(source_of - passed).at[2:2 + 2 * pairs:2].set(sink + passed)
    return lengths[jax.random.permutation(jax.random.fold_in(rng, 2), count)]


def bell_draw(own_key, dims, width, limit, cuts=(), kind=jnp.bfloat16):
    values = width * jax.random.normal(own_key, dims, jnp.float32)
    if cuts:
        values = values * levels(own_key, dims, cuts, -0.22, 0.18)
    return jnp.clip(values, -limit, limit).astype(kind)


def setup_inputs(seed: int = 0) -> dict:
    arg_keys = jax.random.split(jax.random.key(seed), 7)
    return {
        "queries": draw_queries(jax.random.fold_in(arg_keys[6], 71), 0),
        "key_codes": bell_draw(arg_keys[1], (SEQS, SEQ_LEN, D), 1.0, 6.0, ((1, 256),)),
        "key_scales": jnp.clip(jnp.exp(math.log(2.0) - 1.3862944 * jax.random.uniform(arg_keys[2], (SEQS, SEQ_LEN, H), jnp.float32) ** levels(arg_keys[2], (SEQS, SEQ_LEN, H), ((1, 256),), -0.2, 0.2)), 0.5, 2.0).astype(jnp.bfloat16),
        "value_codes": bell_draw(arg_keys[3], (SEQS, SEQ_LEN, D), 1.0, 6.0, ((1, 256),)),
        "value_scales": jnp.clip(jnp.exp(math.log(2.0) - 1.3862944 * jax.random.uniform(arg_keys[4], (SEQS, SEQ_LEN, H), jnp.float32) ** levels(arg_keys[4], (SEQS, SEQ_LEN, H), ((1, 256),), -0.2, 0.2)), 0.5, 2.0).astype(jnp.bfloat16),
        "doc_lengths": jax.vmap(lambda own: ragged(own, NDOC, SEQ_LEN, SEQ_LEN // 2, 2))(jax.random.split(arg_keys[5], SEQS)).reshape((SEQS, NDOC)).astype(jnp.int32),
    }


def hadamard(order):
    index_rows = jnp.arange(order, dtype=jnp.int32)
    intersection = index_rows[:, None] & index_rows[None, :]
    parity = jnp.zeros((order, order), jnp.int32)
    for shift_count in range(order.bit_length()):
        parity = parity + ((intersection >> shift_count) & 1)
    return (1 - 2 * (parity % 2)).astype(jnp.bfloat16)


def dequantize(codes, scales):
    head_dim = codes.shape[-1]
    mixed = jnp.dot(codes.reshape(-1, head_dim), hadamard(head_dim), preferred_element_type=jnp.float32)
    mixed = mixed.reshape(codes.shape) * scales.astype(jnp.float32)[..., None] * (head_dim ** -0.5)
    return mixed.astype(jnp.bfloat16)


def one_sequence(queries, key_codes, key_scales, value_codes, value_scales, doc_lengths):
    length = queries.shape[0]
    keys = dequantize(key_codes.reshape(length, H, DH), key_scales)
    values = dequantize(value_codes.reshape(length, H, DH), value_scales)
    query_heads = queries.reshape(length, H, DH)
    doc_ends = jnp.cumsum(doc_lengths)
    positions = jnp.arange(length, dtype=jnp.int32)
    document = jnp.sum((positions[:, None] >= doc_ends[None, :]).astype(jnp.int32), axis=1)
    block = min(1024, length)
    starts = jnp.arange(0, length, block, dtype=jnp.int32)

    def one_head(head):
        key_head = lax.dynamic_index_in_dim(keys, head, 1, keepdims=False)
        value_head = lax.dynamic_index_in_dim(values, head, 1, keepdims=False)
        query_head = lax.dynamic_index_in_dim(query_heads, head, 1, keepdims=False)

        def one_block(start):
            query_block = lax.dynamic_slice_in_dim(query_head, start, block, 0)
            query_pos = start + jnp.arange(block, dtype=jnp.int32)
            query_doc = lax.dynamic_slice_in_dim(document, start, block, 0)
            scores = jnp.dot(query_block, key_head.T, preferred_element_type=jnp.float32) * (DH ** -0.5)
            allowed = (document[None, :] == query_doc[:, None]) & (positions[None, :] <= query_pos[:, None])
            masked = jnp.where(allowed, scores, -jnp.inf)
            top = jnp.max(masked, axis=1, keepdims=True)
            weights = jnp.where(allowed, jnp.exp(masked - top), 0.0)
            total = jnp.sum(weights, axis=1, keepdims=True)
            numer = jnp.dot(weights.astype(jnp.bfloat16), value_head, preferred_element_type=jnp.float32)
            return (numer / total).astype(jnp.bfloat16)

        return lax.map(one_block, starts).reshape(length, DH)

    result = lax.map(one_head, jnp.arange(H, dtype=jnp.int32))
    return jnp.transpose(result, (1, 0, 2)).reshape(length, H * DH)


def reference(queries, key_codes, key_scales, value_codes, value_scales, doc_lengths):
    outputs = []
    for sequence in range(SEQS):
        outputs.append(one_sequence(queries[sequence], key_codes[sequence], key_scales[sequence],
                                    value_codes[sequence], value_scales[sequence], doc_lengths[sequence]))
    return jnp.stack(outputs, axis=0)
```

```python
import functools
import math

import jax
import jax.numpy as jnp
from jax import lax
from jax.experimental import pallas as pl
from jax.experimental.pallas import tpu as pltpu
from jax.sharding import PartitionSpec as P

MESH = pl.DeviceIdType.MESH
NEG = -1e30
HD = 128
XH, XL, CORES = 2, 2, 2


def place(heads, blocks):
    hc, bc = lax.axis_index("head"), lax.axis_index("blk")
    ny = blocks // (XH * CORES)
    half = ny * CORES
    xh, r = bc // half, lax.rem(bc, half)
    return hc // XL, lax.rem(hc, XL), xh, r // CORES, lax.rem(r, CORES), heads // XL, ny


def z_order(nz):
    order = [0]
    for d in range(1, nz // 2 + 1):
        order.append(d)
        if nz - d != d:
            order.append(nz - d)
    return order


def hadamard_matrix():
    both = lax.broadcasted_iota(jnp.int32, (HD, HD), 0) & lax.broadcasted_iota(jnp.int32, (HD, HD), 1)
    parity = jnp.zeros((HD, HD), jnp.int32)
    for shift in range(7):
        parity = parity + ((both >> shift) & 1)
    return (1 - 2 * (parity & 1)).astype(jnp.float32).astype(jnp.bfloat16)


def spread_kernel(heads, blocks, q_hbm, kc_ref, ks_ref, vc_ref, vs_ref, kv_out, q_out,
                  stage, send_kv, send_q, recv_kv, recv_q, send_y, recv_y, send_r, recv_r, send_s, recv_s, own_sem):
    z, xl, xh, y, c, nz, ny = place(heads, blocks)
    seqs, tok = kc_ref.shape[0], kc_ref.shape[1]
    order = z_order(nz)
    half = ny * CORES

    def dev(z_, xl_, xh_, y_, c_):
        return (z_ * XL + xl_, xh_ * half + y_ * CORES + c_)

    up, down = lax.rem(y + 1, ny), lax.rem(y + ny - 1, ny)
    partners = []
    for dz in order:
        for dl in range(XL):
            for dh in range(XH):
                if (dz, dl, dh) != (0, 0, 0):
                    partners.append((dz, dl, dh))
    barrier = pltpu.get_barrier_semaphore()
    targets = [dev(lax.rem(z + dz, nz), xl ^ dl, xh ^ dh, y, c) for dz, dl, dh in partners]
    targets += [dev(z, xl, xh, up, c), dev(z, xl, xh, down, c), dev(z, xl, xh, y, 1 - c)]
    for t in targets:
        pl.semaphore_signal(barrier, inc=1, device_id=t, device_id_type=MESH)

    had = hadamard_matrix()
    for which, (codes, scales) in enumerate(((kc_ref, ks_ref), (vc_ref, vs_ref))):
        for h in range(heads):
            block = codes[:, :, h * HD:(h + 1) * HD].reshape(seqs * tok, HD)
            mixed = jnp.dot(block, had, preferred_element_type=jnp.float32)
            scale = scales[:, :, h:h + 1].astype(jnp.float32).reshape(seqs * tok, 1)
            mixed = mixed * scale * HD ** (-0.5)
            stage[:, h, which] = mixed.astype(jnp.bfloat16).reshape(seqs, tok, HD)

    pl.semaphore_wait(barrier, len(targets))

    hc = z * XL + xl
    own_kv = pltpu.make_async_copy(stage.at[xh, hc], kv_out.at[hc, xh, y, c], own_sem.at[0])
    own_kv.start()
    own_q = pltpu.make_async_copy(
        q_hbm.at[xh, :, pl.ds(pl.multiple_of(hc * HD, HD), HD)], q_out.at[hc, xh], own_sem.at[1])
    own_q.start()

    def kv_copy(i):
        dz, dl, dh = partners[i]
        tz, tl, th = lax.rem(z + nz - dz, nz), xl ^ dl, xh ^ dh
        return pltpu.make_async_remote_copy(
            src_ref=stage.at[th, tz * XL + tl], dst_ref=kv_out.at[hc, xh, y, c],
            send_sem=send_kv.at[i], recv_sem=recv_kv.at[i],
            device_id=dev(tz, tl, th, y, c), device_id_type=MESH)

    def q_copy(i):
        dz, dl, dh = partners[i]
        tz, tl, th = lax.rem(z + nz - dz, nz), xl ^ dl, xh ^ dh
        return pltpu.make_async_remote_copy(
            src_ref=q_hbm.at[th, :, pl.ds(pl.multiple_of((tz * XL + tl) * HD, HD), HD)],
            dst_ref=q_out.at[hc, xh],
            send_sem=send_q.at[i], recv_sem=recv_q.at[i],
            device_id=dev(tz, tl, th, y, c), device_id_type=MESH)

    kv_copies = [kv_copy(i) for i in range(len(partners))]
    q_copies = [q_copy(i) for i in range(len(partners))]
    for cp in kv_copies:
        cp.start()
    for cp in q_copies:
        cp.start()

    def part(zs, ya, ca):
        return kv_out.at[pl.ds(zs * XL, XL), :, ya, ca]

    def y_copy(k, way):
        ref = part(lax.rem(z + order[k], nz), y, c)
        return pltpu.make_async_remote_copy(
            src_ref=ref, dst_ref=ref, send_sem=send_y.at[way, k], recv_sem=recv_y.at[way, k],
            device_id=dev(z, xl, xh, up if way == 0 else down, c), device_id_type=MESH)

    def y_in(k, way):
        ref = part(lax.rem(z + order[k], nz), down if way == 0 else up, c)
        return pltpu.make_async_remote_copy(
            src_ref=ref, dst_ref=ref, send_sem=send_y.at[way, k], recv_sem=recv_y.at[way, k],
            device_id=dev(z, xl, xh, up, c), device_id_type=MESH)

    far = lax.rem(y + 2, ny)

    def relay_copy(k, way):
        zs = lax.rem(z + order[k], nz) * XL + way
        ref = kv_out.at[zs, :, down if way == 0 else up, c]
        return pltpu.make_async_remote_copy(
            src_ref=ref, dst_ref=ref, send_sem=send_r.at[way, k], recv_sem=recv_r.at[way, k],
            device_id=dev(z, xl, xh, up if way == 0 else down, c), device_id_type=MESH)

    def relay_in(k, way):
        zs = lax.rem(z + order[k], nz) * XL + way
        ref = kv_out.at[zs, :, far, c]
        return pltpu.make_async_remote_copy(
            src_ref=ref, dst_ref=ref, send_sem=send_r.at[way, k], recv_sem=recv_r.at[way, k],
            device_id=dev(z, xl, xh, up, c), device_id_type=MESH)

    def sib_copy(k, j, ca):
        ref = part(lax.rem(z + order[k], nz), (y, down, up, far)[j], ca)
        return pltpu.make_async_remote_copy(
            src_ref=ref, dst_ref=ref, send_sem=send_s.at[j, k], recv_sem=recv_s.at[j, k],
            device_id=dev(z, xl, xh, y, 1 - c), device_id_type=MESH)

    started = []

    def go(cp):
        cp.start()
        started.append(cp)

    per = XL * XH
    for step in range(nz + 2):
        if step < nz:
            k = step
            for i in range(max(0, k * per - 1), (k + 1) * per - 1):
                kv_copies[i].wait_recv()
            if k == 0:
                own_kv.wait()
            go(y_copy(k, 0))
            go(y_copy(k, 1))
            go(sib_copy(k, 0, c))
        if 1 <= step < nz + 1:
            k = step - 1
            for way in range(2):
                y_in(k, way).wait_recv()
                go(relay_copy(k, way))
                go(sib_copy(k, 1 + way, c))
        if step >= 2:
            k = step - 2
            relay_in(k, 0).wait_recv()
            relay_in(k, 1).wait_recv()
            go(sib_copy(k, 3, c))
    for k in range(nz):
        for j in range(4):
            sib_copy(k, j, 1 - c).wait_recv()
    for cp in q_copies:
        cp.wait_recv()
    own_q.wait()
    for cp in kv_copies + q_copies + started:
        cp.wait_send()


def spread(heads, blocks, q, kc, ks, vc, vs):
    seqs, tok, width = q.shape
    nz, ny = heads // XL, blocks // (XH * CORES)
    np_ = nz * XL * XH - 1
    dma = pltpu.SemaphoreType.DMA
    vm, hbm = pl.BlockSpec(memory_space=pltpu.VMEM), pl.BlockSpec(memory_space=pl.ANY)
    return pl.pallas_call(
        functools.partial(spread_kernel, heads, blocks),
        out_shape=(
            jax.ShapeDtypeStruct((heads, XH, ny, CORES, 2, tok, HD), jnp.bfloat16),
            jax.ShapeDtypeStruct((heads, XH, tok, HD), jnp.bfloat16),
        ),
        in_specs=[hbm, vm, vm, vm, vm],
        out_specs=(hbm, hbm),
        scratch_shapes=[
            pltpu.VMEM((seqs, heads, 2, tok, HD), jnp.bfloat16),
            dma((np_,)), dma((np_,)), dma((np_,)), dma((np_,)),
            dma((2, nz)), dma((2, nz)), dma((2, nz)), dma((2, nz)),
            dma((4, nz)), dma((4, nz)), dma((2,)),
        ],
        compiler_params=pltpu.CompilerParams(
            collective_id=0, has_side_effects=True, vmem_limit_bytes=48 * 1024 * 1024),
    )(q, kc, ks, vc, vs)


def back_kernel(heads, blocks, o_hbm, out_hbm, send, recv, own_sem):
    z, xl, xh, y, c, nz, ny = place(heads, blocks)
    half = ny * CORES
    hc = z * XL + xl

    def dev(z_, xl_, xh_):
        return (z_ * XL + xl_, xh_ * half + y * CORES + c)

    partners = [(dz, dl, dh) for dz in z_order(nz)[::-1] for dl in range(XL) for dh in range(XH)
                if (dz, dl, dh) != (0, 0, 0)]
    barrier = pltpu.get_barrier_semaphore()
    for dz, dl, dh in partners:
        pl.semaphore_signal(barrier, inc=1, device_id=dev(lax.rem(z + dz, nz), xl ^ dl, xh ^ dh), device_id_type=MESH)
    pl.semaphore_wait(barrier, len(partners))
    mine = out_hbm.at[xh, :, pl.ds(pl.multiple_of(hc * HD, HD), HD)]
    copies = []
    for i, (dz, dl, dh) in enumerate(partners):
        tz, tl, th = lax.rem(z + nz - dz, nz), xl ^ dl, xh ^ dh
        cp = pltpu.make_async_remote_copy(
            src_ref=o_hbm.at[tz * XL + tl, th], dst_ref=mine,
            send_sem=send.at[i], recv_sem=recv.at[i], device_id=dev(tz, tl, th), device_id_type=MESH)
        cp.start()
        copies.append(cp)
    own = pltpu.make_async_copy(o_hbm.at[hc, xh], mine, own_sem)
    own.start()
    own.wait()
    for cp in copies:
        cp.wait_recv()
    for cp in copies:
        cp.wait_send()


def back(heads, blocks, o, tok, seqs):
    n = heads * XH - 1
    dma = pltpu.SemaphoreType.DMA
    hbm = pl.BlockSpec(memory_space=pl.ANY)
    return pl.pallas_call(
        functools.partial(back_kernel, heads, blocks),
        out_shape=jax.ShapeDtypeStruct((seqs, tok, heads * HD), jnp.bfloat16),
        in_specs=[hbm],
        out_specs=hbm,
        scratch_shapes=[dma((n,)), dma((n,)), dma],
        compiler_params=pltpu.CompilerParams(
            collective_id=1, has_side_effects=True, vmem_limit_bytes=48 * 1024 * 1024),
    )(o)


def attn_kernel(ns, CK, variant, meta_ref, q_ref, kv_hbm, o_ref, kv_v, s_ref, sems):
    ndoc = 8
    U = q_ref.shape[0]
    T = q_ref.shape[1]
    TQ = ns * T
    tiles = U // ns
    period = kv_hbm.shape[0] // U * T
    nload = sems.shape[0]
    per = kv_hbm.shape[0] // nload
    tiles_per = tiles // nload
    c = math.log2(math.e) / math.sqrt(128.0)
    for i in range(nload):
        pltpu.make_async_copy(kv_hbm.at[pl.ds(i * per, per)], kv_v.at[pl.ds(i * per, per)], sems.at[i]).start()
    r = meta_ref[ndoc]
    ends = [meta_ref[i] for i in range(ndoc)]

    def start_of(p):
        out = jnp.int32(0)
        for e in ends:
            out = jnp.maximum(out, jnp.where(e <= p, e, 0))
        return out

    kdim = 0 if variant == "T" else 1
    rows_shape = (8, TQ) if variant == "T" else (TQ, 128)

    def tile(t, _):
        @pl.when(lax.rem(t, tiles_per) == 0)
        def _():
            i = t // tiles_per
            pltpu.make_async_copy(kv_hbm.at[pl.ds(i * per, per)], kv_v.at[pl.ds(i * per, per)], sems.at[i]).wait()
        q = q_ref[pl.ds(t * ns, ns)].reshape(TQ, 128)
        p_first = t * (ns * period) + r * T
        p_last = p_first + (ns - 1) * period + T - 1
        st_first = start_of(p_first)
        st_last = start_of(p_last)
        c_lo = st_first // CK
        c_end = p_last // CK + 1
        f_lo = jnp.clip((st_last + CK - 1) // CK, c_lo, c_end)
        f_hi = jnp.maximum(f_lo, (p_first + 1) // CK)
        ridx = lax.broadcasted_iota(jnp.int32, rows_shape, 1 - kdim)
        qpos = p_first + (ridx // T) * period + ridx % T
        ds = jnp.zeros(rows_shape, jnp.int32)
        for e in ends:
            ds = jnp.maximum(ds, jnp.where(qpos >= e, e, 0))
        kidx = lax.broadcasted_iota(jnp.int32, rows_shape, kdim)
        dsr = ds - kidx
        qpr = qpos - kidx
        step = 8 if variant == "T" else 128

        def p1(ck, m, masked):
            k = kv_v[pl.ds(ck * (CK // T), CK // T), 0].reshape(CK, 128)
            if variant == "T":
                s = lax.dot_general(k, q, (((1,), (1,)), ((), ())), preferred_element_type=jnp.float32)
            else:
                s = lax.dot_general(q, k, (((1,), (1,)), ((), ())), preferred_element_type=jnp.float32)
            for j in range(CK // step):
                if variant == "T":
                    sj = s[j * 8:(j + 1) * 8]
                else:
                    sj = s[:, j * 128:(j + 1) * 128]
                if masked:
                    base = ck * CK + j * step
                    sj = jnp.where((base >= dsr) & (base <= qpr), sj, NEG)
                if variant == "T":
                    s_ref[ck - c_lo, pl.ds(j * 8, 8), :] = sj
                else:
                    s_ref[ck - c_lo, :, pl.ds(j * 128, 128)] = sj
                m = jnp.maximum(m, sj)
            return m

        m = jnp.full(rows_shape, NEG, jnp.float32)
        m = lax.fori_loop(c_lo, f_lo, lambda i, m: p1(i, m, True), m)
        m = lax.fori_loop(f_lo, f_hi, lambda i, m: p1(i, m, False), m)
        m = lax.fori_loop(f_hi, c_end, lambda i, m: p1(i, m, True), m)
        mc = jnp.broadcast_to(jnp.max(m, axis=kdim, keepdims=True) * c, rows_shape)

        def p2(ck, carry):
            l, acc = carry
            v = kv_v[pl.ds(ck * (CK // T), CK // T), 1].reshape(CK, 128)
            ps = []
            for j in range(CK // step):
                if variant == "T":
                    sj = s_ref[ck - c_lo, pl.ds(j * 8, 8), :]
                else:
                    sj = s_ref[ck - c_lo, :, pl.ds(j * 128, 128)]
                p = jnp.exp2(sj * c - mc)
                l = l + p
                ps.append(p)
            if variant == "T":
                pb = jnp.concatenate(ps, 0).astype(jnp.bfloat16)
                acc = acc + lax.dot_general(v, pb, (((0,), (0,)), ((), ())), preferred_element_type=jnp.float32)
            else:
                pb = jnp.concatenate(ps, 1).astype(jnp.bfloat16)
                acc = acc + jnp.dot(pb, v, preferred_element_type=jnp.float32)
            return l, acc

        acc0 = jnp.zeros((128, TQ) if variant == "T" else (TQ, 128), jnp.float32)
        l, acc = lax.fori_loop(c_lo, c_end, p2, (jnp.zeros(rows_shape, jnp.float32), acc0))
        tot = jnp.sum(l, axis=kdim, keepdims=True)
        o = acc / tot
        if variant == "T":
            o = o.T
        o_ref[pl.ds(t * ns, ns)] = o.astype(jnp.bfloat16).reshape(ns, T, 128)
        return 0

    lax.fori_loop(0, tiles, tile, 0)


def attend(meta, q, kv, ns=2, CK=512, variant="N"):
    U, T = q.shape[:2]
    TQ = ns * T
    period = kv.shape[0] // U * T
    seq = kv.shape[0] * T
    nch = (seq // 2 + ns * period) // CK + 2
    sshape = (nch, CK, TQ) if variant == "T" else (nch, TQ, CK)
    return pl.pallas_call(
        functools.partial(attn_kernel, ns, CK, variant),
        out_shape=jax.ShapeDtypeStruct(q.shape, jnp.bfloat16),
        in_specs=[pl.BlockSpec(memory_space=pltpu.SMEM), pl.BlockSpec(memory_space=pltpu.VMEM), pl.BlockSpec(memory_space=pl.ANY)],
        out_specs=pl.BlockSpec(memory_space=pltpu.VMEM),
        scratch_shapes=[
            pltpu.VMEM(kv.shape, jnp.bfloat16),
            pltpu.VMEM(sshape, jnp.float32),
            pltpu.SemaphoreType.DMA((min(8, U // ns),)),
        ],
        compiler_params=pltpu.CompilerParams(vmem_limit_bytes=48 * 1024 * 1024),
    )(meta, q, kv)


def body(heads, blocks, queries, key_codes, key_scales, value_codes, value_scales, doc_lengths):
    seqs, tok, _ = queries.shape
    ny = blocks // (XH * CORES)
    half = ny * CORES
    kv, q = spread(heads, blocks, queries, key_codes, key_scales, value_codes, value_scales)
    bc = lax.axis_index("blk")
    ends = jnp.cumsum(doc_lengths, axis=1)
    mine = lax.dynamic_index_in_dim(ends, bc // half, 0, keepdims=False)
    meta = jnp.concatenate([mine, jnp.reshape(bc % half, (1,))]).astype(jnp.int32)
    o = attend(meta, q.reshape(heads * XH, tok, HD), kv.reshape(heads * blocks, 2, tok, HD), ns=4, CK=2048, variant="T")
    return back(heads, blocks, o.reshape(heads, XH, tok, HD), tok, seqs)


def solution(mesh):
    rows = P(None, ("head", "blk"), None)
    return jax.shard_map(
        functools.partial(body, mesh.shape["head"], mesh.shape["blk"]),
        mesh=mesh,
        in_specs=(rows, rows, rows, rows, rows, P()),
        out_specs=rows,
        check_vma=False,
    )
```

```python
import functools
import math

import jax
import jax.numpy as jnp
from jax import lax
from jax.experimental import pallas as pl
from jax.experimental.pallas import tpu as pltpu
from jax.sharding import PartitionSpec as P

MESH = pl.DeviceIdType.MESH
NEG = -1e30
LEAST = -(1 << 31)
VMEM_ASK = 60 * 1024 * 1024
HD = 128
XH, XL, CORES = 2, 2, 2


def place(heads, blocks):
    hc, bc = lax.axis_index("head"), lax.axis_index("blk")
    ny = blocks // (XH * CORES)
    half = ny * CORES
    xh, r = bc // half, lax.rem(bc, half)
    return hc // XL, lax.rem(hc, XL), xh, r // CORES, lax.rem(r, CORES), heads // XL, ny


def z_order(nz):
    order = [0]
    for d in range(1, nz // 2 + 1):
        order.append(d)
        if nz - d != d:
            order.append(nz - d)
    return order


def hadamard_matrix():
    both = lax.broadcasted_iota(jnp.int32, (HD, HD), 0) & lax.broadcasted_iota(jnp.int32, (HD, HD), 1)
    parity = jnp.zeros((HD, HD), jnp.int32)
    for shift in range(7):
        parity = parity + ((both >> shift) & 1)
    return (1 - 2 * (parity & 1)).astype(jnp.float32).astype(jnp.bfloat16)


def spread_kernel(heads, blocks, q_hbm, kc_hbm, ks_ref, vc_hbm, vs_ref, kv_out, q_out,
                  codes, wide, stage, send_kv, send_q, recv_kv, recv_q, send_y, recv_y, send_r, recv_r, send_s, recv_s, own_sem):
    z, xl, xh, y, c, nz, ny = place(heads, blocks)
    seqs, tok = kc_hbm.shape[0], kc_hbm.shape[1]
    half = ny * CORES
    loads = [pltpu.make_async_copy(ref, codes.at[i], own_sem.at[2 + i]) for i, ref in enumerate((kc_hbm, vc_hbm))]
    for cp in loads:
        cp.start()

    def dev(z_, xl_, xh_, y_, c_):
        return (z_ * XL + xl_, xh_ * half + y_ * CORES + c_)

    up, down, far = lax.rem(y + 1, ny), lax.rem(y + ny - 1, ny), lax.rem(y + 2, ny)
    groups = [[0]] + [sorted({d, nz - d}) for d in range(1, nz // 2 + 1)]
    order = [dz for group in groups for dz in group]
    partners = [(dz, dl, dh) for dz in order for dl in range(XL) for dh in range(XH) if (dz, dl, dh) != (0, 0, 0)]
    barrier = pltpu.get_barrier_semaphore()
    targets = [dev(lax.rem(z + dz, nz), xl ^ dl, xh ^ dh, y, c) for dz, dl, dh in partners]
    targets += [dev(z, xl, xh, up, c), dev(z, xl, xh, down, c), dev(z, xl, xh, y, 1 - c)]
    for t in targets:
        pl.semaphore_signal(barrier, inc=1, device_id=t, device_id_type=MESH)

    had = hadamard_matrix()
    head_of_lane = lax.broadcasted_iota(jnp.int32, (heads, heads * HD), 1) // HD
    pick = jnp.where(head_of_lane == lax.broadcasted_iota(jnp.int32, (heads, heads * HD), 0), 1.0, 0.0).astype(jnp.bfloat16)
    for which, scales in enumerate((ks_ref, vs_ref)):
        for n in range(seqs):
            wide[which, n] = lax.dot_general(
                scales[n], pick, (((0,), (0,)), ((), ())), preferred_element_type=jnp.float32) * HD ** (-0.5)
        loads[which].wait()

    def dequantize(dz):
        for which in range(2):
            for l in range(XL):
                h = lax.rem(z + nz - dz, nz) * XL + l
                cols = pl.ds(pl.multiple_of(h * HD, HD), HD)
                mixed = jnp.dot(codes[which, :, :, cols].reshape(seqs * tok, HD), had, preferred_element_type=jnp.float32)
                for n in range(seqs):
                    stage[n, h, which] = (mixed[n * tok:(n + 1) * tok] * wide[which, n, :, cols]).astype(jnp.bfloat16)

    dequantize(0)
    pl.semaphore_wait(barrier, len(targets))

    hc = z * XL + xl
    own_kv = pltpu.make_async_copy(stage.at[xh, hc], kv_out.at[hc, xh, y, c], own_sem.at[0])
    own_kv.start()
    own_q = pltpu.make_async_copy(
        q_hbm.at[xh, :, pl.ds(pl.multiple_of(hc * HD, HD), HD)], q_out.at[hc, xh], own_sem.at[1])
    own_q.start()

    def kv_copy(i):
        dz, dl, dh = partners[i]
        tz, tl, th = lax.rem(z + nz - dz, nz), xl ^ dl, xh ^ dh
        return pltpu.make_async_remote_copy(
            src_ref=stage.at[th, tz * XL + tl], dst_ref=kv_out.at[hc, xh, y, c],
            send_sem=send_kv.at[i], recv_sem=recv_kv.at[i],
            device_id=dev(tz, tl, th, y, c), device_id_type=MESH)

    def q_copy(i):
        dz, dl, dh = partners[i]
        tz, tl, th = lax.rem(z + nz - dz, nz), xl ^ dl, xh ^ dh
        return pltpu.make_async_remote_copy(
            src_ref=q_hbm.at[th, :, pl.ds(pl.multiple_of((tz * XL + tl) * HD, HD), HD)],
            dst_ref=q_out.at[hc, xh],
            send_sem=send_q.at[i], recv_sem=recv_q.at[i],
            device_id=dev(tz, tl, th, y, c), device_id_type=MESH)

    kv_copies = [kv_copy(i) for i in range(len(partners))]
    q_copies = [q_copy(i) for i in range(len(partners))]

    def kv_of(g):
        return [cp for p, cp in zip(partners, kv_copies) if p[0] in groups[g]]

    def part(zs, ya, ca):
        return kv_out.at[pl.ds(zs * XL, XL), :, ya, ca]

    def y_copy(dz, way, incoming=False):
        ref = part(lax.rem(z + dz, nz), (down if way == 0 else up) if incoming else y, c)
        k = order.index(dz)
        return pltpu.make_async_remote_copy(
            src_ref=ref, dst_ref=ref, send_sem=send_y.at[way, k], recv_sem=recv_y.at[way, k],
            device_id=dev(z, xl, xh, up if way == 0 else down, c), device_id_type=MESH)

    def relay_copy(dz, way, incoming=False):
        zs = lax.rem(z + dz, nz) * XL + way
        k = order.index(dz)
        ref = kv_out.at[zs, :, far if incoming else (down if way == 0 else up), c]
        return pltpu.make_async_remote_copy(
            src_ref=ref, dst_ref=ref, send_sem=send_r.at[way, k], recv_sem=recv_r.at[way, k],
            device_id=dev(z, xl, xh, up if way == 0 else down, c), device_id_type=MESH)

    def sib_copy(dz, j, ca):
        ref = part(lax.rem(z + dz, nz), (y, down, up, far)[j], ca)
        k = order.index(dz)
        return pltpu.make_async_remote_copy(
            src_ref=ref, dst_ref=ref, send_sem=send_s.at[j, k], recv_sem=recv_s.at[j, k],
            device_id=dev(z, xl, xh, y, 1 - c), device_id_type=MESH)

    started = []

    def go(cp):
        cp.start()
        started.append(cp)

    for g in range(len(groups)):
        if g:
            for dz in groups[g]:
                dequantize(dz)
        if g < 3:
            for cp in kv_of(g):
                go(cp)
    for step in range(len(groups) + 2):
        if step < len(groups):
            for cp in kv_of(step):
                cp.wait_recv()
            if step == 0:
                own_kv.wait()
            for dz in groups[step]:
                go(y_copy(dz, 0))
                go(y_copy(dz, 1))
            if 1 <= step and step + 2 < len(groups):
                for cp in kv_of(step + 2):
                    go(cp)
            if step == len(groups) - 1:
                for cp in q_copies:
                    go(cp)
            for dz in groups[step]:
                go(sib_copy(dz, 0, c))
        if 1 <= step < len(groups) + 1:
            for dz in groups[step - 1]:
                for way in range(2):
                    y_copy(dz, way, True).wait_recv()
                    go(relay_copy(dz, way))
                    go(sib_copy(dz, 1 + way, c))
        if step >= 2:
            for dz in groups[step - 2]:
                relay_copy(dz, 0, True).wait_recv()
                relay_copy(dz, 1, True).wait_recv()
                go(sib_copy(dz, 3, c))
    for dz in order:
        for j in range(4):
            sib_copy(dz, j, 1 - c).wait_recv()
    for cp in q_copies:
        cp.wait_recv()
    own_q.wait()
    for cp in started:
        cp.wait_send()


def spread(heads, blocks, q, kc, ks, vc, vs):
    seqs, tok, width = q.shape
    nz, ny = heads // XL, blocks // (XH * CORES)
    np_ = nz * XL * XH - 1
    dma = pltpu.SemaphoreType.DMA
    vm, hbm = pl.BlockSpec(memory_space=pltpu.VMEM), pl.BlockSpec(memory_space=pl.ANY)
    return pl.pallas_call(
        functools.partial(spread_kernel, heads, blocks),
        out_shape=(
            jax.ShapeDtypeStruct((heads, XH, ny, CORES, 2, tok, HD), jnp.bfloat16),
            jax.ShapeDtypeStruct((heads, XH, tok, HD), jnp.bfloat16),
        ),
        in_specs=[hbm, hbm, vm, hbm, vm],
        out_specs=(hbm, hbm),
        scratch_shapes=[
            pltpu.VMEM((2, seqs, tok, heads * HD), jnp.bfloat16),
            pltpu.VMEM((2, seqs, tok, heads * HD), jnp.float32),
            pltpu.VMEM((seqs, heads, 2, tok, HD), jnp.bfloat16),
            dma((np_,)), dma((np_,)), dma((np_,)), dma((np_,)),
            dma((2, nz)), dma((2, nz)), dma((2, nz)), dma((2, nz)),
            dma((4, nz)), dma((4, nz)), dma((4,)),
        ],
        compiler_params=pltpu.CompilerParams(
            collective_id=0, has_side_effects=True, vmem_limit_bytes=VMEM_ASK),
    )(q, kc, jnp.transpose(ks, (0, 2, 1)), vc, jnp.transpose(vs, (0, 2, 1)))


def back_kernel(heads, blocks, o_hbm, out_hbm, send, recv, own_sem):
    z, xl, xh, y, c, nz, ny = place(heads, blocks)
    half = ny * CORES
    hc = z * XL + xl

    def dev(z_, xl_, xh_):
        return (z_ * XL + xl_, xh_ * half + y * CORES + c)

    partners = [(dz, dl, dh) for dz in z_order(nz)[::-1] for dl in range(XL) for dh in range(XH)
                if (dz, dl, dh) != (0, 0, 0)]
    barrier = pltpu.get_barrier_semaphore()
    for dz, dl, dh in partners:
        pl.semaphore_signal(barrier, inc=1, device_id=dev(lax.rem(z + dz, nz), xl ^ dl, xh ^ dh), device_id_type=MESH)
    pl.semaphore_wait(barrier, len(partners))
    mine = out_hbm.at[xh, :, pl.ds(pl.multiple_of(hc * HD, HD), HD)]
    copies = []
    for i, (dz, dl, dh) in enumerate(partners):
        tz, tl, th = lax.rem(z + nz - dz, nz), xl ^ dl, xh ^ dh
        cp = pltpu.make_async_remote_copy(
            src_ref=o_hbm.at[tz * XL + tl, th], dst_ref=mine,
            send_sem=send.at[i], recv_sem=recv.at[i], device_id=dev(tz, tl, th), device_id_type=MESH)
        cp.start()
        copies.append(cp)
    own = pltpu.make_async_copy(o_hbm.at[hc, xh], mine, own_sem)
    own.start()
    own.wait()
    for cp in copies:
        cp.wait_recv()
    for cp in copies:
        cp.wait_send()


def back(heads, blocks, o, tok, seqs):
    n = heads * XH - 1
    dma = pltpu.SemaphoreType.DMA
    hbm = pl.BlockSpec(memory_space=pl.ANY)
    return pl.pallas_call(
        functools.partial(back_kernel, heads, blocks),
        out_shape=jax.ShapeDtypeStruct((seqs, tok, heads * HD), jnp.bfloat16),
        in_specs=[hbm],
        out_specs=hbm,
        scratch_shapes=[dma((n,)), dma((n,)), dma],
        compiler_params=pltpu.CompilerParams(
            collective_id=1, has_side_effects=True, vmem_limit_bytes=VMEM_ASK),
    )(o)


def attn_kernel(ns, CK, ring, half, doc_ref, q_ref, kv_hbm, o_ref, kv_v, s_a, s_b, p_a, p_b, acc_ref,
                mc_ref, l_ref, lo_ref, len_ref, tile_of, chunk_of, flag_of, sems):
    ndoc = doc_ref.shape[1]
    U, T = q_ref.shape[:2]
    TQ = ns * T
    tiles = U // ns
    period = kv_hbm.shape[0] // U * T
    nload = sems.shape[0]
    per = kv_hbm.shape[0] // nload
    tiles_per = tiles // nload
    CR = CK // T
    c = math.log2(math.e) / math.sqrt(float(HD))
    for i in range(nload):
        pltpu.make_async_copy(kv_hbm.at[pl.ds(i * per, per)], kv_v.at[pl.ds(i * per, per)], sems.at[i]).start()
    bc = lax.axis_index("blk")
    own_seq, r = bc // half, lax.rem(bc, half)
    ends = []
    for i in range(ndoc):
        ends.append(doc_ref[own_seq, i] + (ends[-1] if ends else 0))

    def start_of(p):
        out = jnp.int32(0)
        for e in ends:
            out = jnp.maximum(out, jnp.where(e <= p, e, 0))
        return out

    lane = lax.broadcasted_iota(jnp.int32, (8, TQ), 1)
    sub = lax.broadcasted_iota(jnp.int32, (8, TQ), 0)

    def first_of(t):
        return t * (ns * period) + r * T

    lead = ring + 2

    def blank(i, _):
        tile_of[i] = tiles
        chunk_of[i] = 0
        flag_of[i] = 0
        return 0

    def add_tile(t, carry):
        n, longest = carry
        p_first = first_of(t)
        p_last = p_first + (ns - 1) * period + T - 1
        c_lo = start_of(p_first) // CK
        c_end = p_last // CK + 1
        qpos = p_first + (lane // T) * period + lax.rem(lane, T)
        ds = jnp.zeros((8, TQ), jnp.int32)
        for e in ends:
            ds = jnp.maximum(ds, jnp.where(qpos >= e, e, 0))
        lo_ref[t] = sub - ds + LEAST
        len_ref[t] = qpos - ds + LEAST

        def add(ck, n):
            tile_of[lead + n] = t
            chunk_of[lead + n] = ck
            flag_of[lead + n] = jnp.where(ck == c_lo, 1, 0) + jnp.where(ck == c_end - 1, 2, 0)
            return n + 1

        return lax.fori_loop(c_lo, c_end, add, n), jnp.maximum(longest, c_end - c_lo)

    lax.fori_loop(0, lead, blank, 0)
    count, longest = lax.fori_loop(0, tiles, add_tile, (jnp.int32(0), jnp.int32(0)))
    lag = longest | 1
    lax.fori_loop(lead + count, lead + count + lag + 3, blank, 0)
    lo_ref[tiles] = jnp.zeros((8, TQ), jnp.int32)
    len_ref[tiles] = jnp.zeros((8, TQ), jnp.int32)
    mc_ref[tiles] = jnp.zeros((8, TQ), jnp.float32)
    acc_ref[tiles] = jnp.zeros((HD, TQ), jnp.float32)
    SB = min(256, CK)
    PB = min(512, CK)

    def scores(j, m, s_w):
        tj, fj = tile_of[lead + j], flag_of[lead + j]
        slot = lax.rem(j // 2, ring)
        k_at = chunk_of[lead + j] * CR
        q = q_ref[pl.ds(jnp.minimum(tj, tiles - 1) * ns, ns)].reshape(TQ, HD)
        lo, ln = lo_ref[tj] + chunk_of[lead + j] * CK, len_ref[tj]
        ms = [jnp.where((fj & 1) == 1, NEG, m)] * 2

        def piece(b):
            k = kv_v[pl.ds(k_at + b * (SB // T), SB // T), 0].reshape(SB, HD)
            s = lax.dot_general(k, q, (((1,), (1,)), ((), ())), preferred_element_type=jnp.float32)
            for i in range(SB // 8):
                si = jnp.where(lo + (b * SB + i * 8) <= ln, s[i * 8:(i + 1) * 8], NEG)
                s_w[slot, pl.ds(b * SB + i * 8, 8), :] = si
                ms[i % 2] = jnp.maximum(ms[i % 2], si)

        def finish():
            m = jnp.maximum(ms[0], ms[1])
            mc_ref[tj] = jnp.broadcast_to(jnp.max(m, axis=0, keepdims=True) * c, (8, TQ))
            return m

        return piece, finish

    def weights(e, l, s_r, p_w):
        te, fe = tile_of[lead + e], flag_of[lead + e]
        slot = lax.rem(jnp.maximum(e, 0) // 2, ring)
        mc = mc_ref[te]
        ls = [jnp.where((fe & 1) == 1, 0.0, l), jnp.zeros((8, TQ), jnp.float32)]

        def piece(b):
            prev = None
            for i in range(SB // 8):
                p = jnp.exp2(s_r[slot, pl.ds(b * SB + i * 8, 8), :] * c - mc)
                ls[i % 2] = ls[i % 2] + p
                if i % 2:
                    p_w[pl.ds(b * SB + (i - 1) * 8, 16), :] = jnp.concatenate([prev, p], 0).astype(jnp.bfloat16)
                prev = p

        def finish():
            l = ls[0] + ls[1]
            l_ref[te] = l
            return l

        return piece, finish

    def products(g, p_r):
        tg, fg = tile_of[lead + g], flag_of[lead + g]
        v_at = chunk_of[lead + g] * CR
        acc = [jnp.where((fg & 1) == 1, 0.0, acc_ref[tg])]

        def piece(b):
            if (b + 1) * SB % PB:
                return
            at = (b + 1) * SB - PB
            v = kv_v[pl.ds(v_at + at // T, PB // T), 1].reshape(PB, HD)
            acc[0] = acc[0] + lax.dot_general(
                v, p_r[pl.ds(at, PB), :], (((0,), (0,)), ((), ())), preferred_element_type=jnp.float32)

        def finish():
            acc_ref[tg] = acc[0]

        return piece, finish

    def bring(j):
        t = tile_of[lead + j]

        @pl.when(((flag_of[lead + j] & 1) == 1) & (lax.rem(t, tiles_per) == 0))
        def _():
            i = t // tiles_per
            pltpu.make_async_copy(kv_hbm.at[pl.ds(i * per, per)], kv_v.at[pl.ds(i * per, per)], sems.at[i]).wait()

    def half_step(first, last, j, m, l, s_w, s_r, p_w, p_r):
        parts = []
        if not last:
            parts.append(scores(j, m, s_w))
        if not first:
            parts.append(weights(j - lag, l, s_r, p_w))
            parts.append(products(j - lag - 1, p_r))
        for b in range(CK // SB):
            for piece, _ in parts:
                piece(b)
        if not last:
            m = parts[0][1]()
        if not first:
            l = parts[-2][1]()
            parts[-1][1]()
        return m, l

    def two(first, last, i, carry):
        m, l = carry
        if not last:
            bring(2 * i)
            bring(2 * i + 1)
        m, l = half_step(first, last, 2 * i, m, l, s_a, s_b, p_a, p_b)
        m, l = half_step(first, last, 2 * i + 1, m, l, s_b, s_a, p_b, p_a)
        return m, l

    zero = jnp.zeros((8, TQ), jnp.float32)
    begin, full, end = lag // 2, (count + 1) // 2, (count + lag + 2) // 2
    begin = jnp.minimum(begin, full)
    carry = lax.fori_loop(0, begin, functools.partial(two, True, False), (zero, zero))
    carry = lax.fori_loop(begin, full, functools.partial(two, False, False), carry)
    lax.fori_loop(full, end, functools.partial(two, False, True), carry)

    def close(t, _):
        total = jnp.sum(l_ref[t], axis=0, keepdims=True)
        o = (acc_ref[t] / total).T
        o_ref[pl.ds(t * ns, ns)] = o.astype(jnp.bfloat16).reshape(ns, T, HD)
        return 0

    lax.fori_loop(0, tiles, close, 0)


def attend(blocks, docs, q, kv, ns=4, CK=1024):
    U, T = q.shape[:2]
    TQ = ns * T
    tiles = U // ns
    period = kv.shape[0] // U * T
    seq = kv.shape[0] * T
    longest = (seq // 2 + ns * period) // CK + 2
    items = tiles * longest
    ring = longest // 2 + 2
    lead = ring + 2
    table = pltpu.SMEM((items + 2 * longest + 16,), jnp.int32)
    per_tile = lambda dt: pltpu.VMEM((tiles + 1, 8, TQ), dt)
    return pl.pallas_call(
        functools.partial(attn_kernel, ns, CK, longest + 2, blocks // 2),
        out_shape=jax.ShapeDtypeStruct(q.shape, jnp.bfloat16),
        in_specs=[pl.BlockSpec(memory_space=pltpu.SMEM), pl.BlockSpec(memory_space=pltpu.VMEM), pl.BlockSpec(memory_space=pl.ANY)],
        out_specs=pl.BlockSpec(memory_space=pltpu.VMEM),
        scratch_shapes=[
            pltpu.VMEM(kv.shape, jnp.bfloat16),
            pltpu.VMEM((longest + 2, CK, TQ), jnp.float32),
            pltpu.VMEM((longest + 2, CK, TQ), jnp.float32),
            pltpu.VMEM((CK, TQ), jnp.bfloat16),
            pltpu.VMEM((CK, TQ), jnp.bfloat16),
            pltpu.VMEM((tiles + 1, HD, TQ), jnp.float32),
            per_tile(jnp.float32), per_tile(jnp.float32), per_tile(jnp.int32), per_tile(jnp.int32),
            table, table, table,
            pltpu.SemaphoreType.DMA((min(8, tiles),)),
        ],
        compiler_params=pltpu.CompilerParams(vmem_limit_bytes=VMEM_ASK),
    )(docs, q, kv)


def body(heads, blocks, queries, key_codes, key_scales, value_codes, value_scales, doc_lengths):
    seqs, tok, _ = queries.shape
    kv, q = spread(heads, blocks, queries, key_codes, key_scales, value_codes, value_scales)
    o = attend(blocks, doc_lengths, q.reshape(heads * XH, tok, HD), kv.reshape(heads * blocks, 2, tok, HD))
    return back(heads, blocks, o.reshape(heads, XH, tok, HD), tok, seqs)


def solution(mesh):
    rows = P(None, ("head", "blk"), None)
    return jax.shard_map(
        functools.partial(body, mesh.shape["head"], mesh.shape["blk"]),
        mesh=mesh,
        in_specs=(rows, rows, rows, rows, rows, P()),
        out_specs=rows,
        check_vma=False,
    )
```

```python
import functools
import math

import jax
import jax.numpy as jnp
from jax import lax
from jax.experimental import pallas as pl
from jax.experimental.pallas import tpu as pltpu
from jax.sharding import PartitionSpec as P

MESH = pl.DeviceIdType.MESH
NEG = -1e30
LEAST = -(1 << 31)
VMEM_ASK = 60 * 1024 * 1024
HD = 128
XH, XL, CORES = 2, 2, 2


def hadamard_matrix():
    both = lax.broadcasted_iota(jnp.int32, (HD, HD), 0) & lax.broadcasted_iota(jnp.int32, (HD, HD), 1)
    parity = jnp.zeros((HD, HD), jnp.int32)
    for shift in range(7):
        parity = parity + ((both >> shift) & 1)
    return (1 - 2 * (parity & 1)).astype(jnp.float32).astype(jnp.bfloat16)


def kernel(heads, blocks, doc_ref, q_hbm, kc_hbm, ks_ref, vc_hbm, vs_ref, out_hbm,
           codes, wide, stage, kv, qv, ov, s_a, s_b, p_a, p_b, acc_ref, m_ref, l_ref, lo_ref, len_ref, mc_ref, ratio_ref,
           send_kv, send_q, send_o, recv_kv, recv_q, recv_o, send_y, recv_y, send_r, recv_r, send_s, recv_s, own_sem):
    nz, ny = heads // XL, blocks // (XH * CORES)
    half = ny * CORES
    hc, bc = lax.axis_index("head"), lax.axis_index("blk")
    z, xl = lax.div(hc, XL), lax.rem(hc, XL)
    xh, r = lax.div(bc, half), lax.rem(bc, half)
    y, c = lax.div(r, CORES), lax.rem(r, CORES)
    seqs, tok = kc_hbm.shape[0], kc_hbm.shape[1]
    TQ = XL * XH * tok
    CK = XH * half * tok
    SB = 2 * CORES * tok
    period = half * tok
    scale = math.log2(math.e) / math.sqrt(float(HD))

    loads = [pltpu.make_async_copy(ref, codes.at[i], own_sem.at[3 + i]) for i, ref in enumerate((kc_hbm, vc_hbm))]
    for cp in loads:
        cp.start()

    def dev(z_, xl_, xh_, y_, c_):
        return (z_ * XL + xl_, xh_ * half + y_ * CORES + c_)

    up, down, far = lax.rem(y + 1, ny), lax.rem(y + ny - 1, ny), lax.rem(y + 2, ny)
    order = [(k + 1) // 2 if k % 2 else (nz - k // 2) % nz for k in range(nz)]
    offsets = [(dl, dh) for dl in range(XL) for dh in range(XH)]
    partners = [(dz, dl, dh) for dz in order for dl, dh in offsets if (dz, dl, dh) != (0, 0, 0)]
    barrier = pltpu.get_barrier_semaphore()
    targets = [dev(lax.rem(z + dz, nz), xl ^ dl, xh ^ dh, y, c) for dz, dl, dh in partners]
    targets += [dev(z, xl, xh, up, c), dev(z, xl, xh, down, c), dev(z, xl, xh, y, 1 - c)]
    for t in targets:
        pl.semaphore_signal(barrier, inc=1, device_id=t, device_id_type=MESH)

    had = hadamard_matrix()
    head_of_lane = lax.broadcasted_iota(jnp.int32, (heads, heads * HD), 1) // HD
    pick = jnp.where(head_of_lane == lax.broadcasted_iota(jnp.int32, (heads, heads * HD), 0), 1.0, 0.0).astype(jnp.bfloat16)
    for which, scales in enumerate((ks_ref, vs_ref)):
        for n in range(seqs):
            wide[which, n] = lax.dot_general(
                scales[n], pick, (((0,), (0,)), ((), ())), preferred_element_type=jnp.float32) * HD ** (-0.5)
        loads[which].wait()

    def dequantize(dz):
        for which in range(2):
            for l in range(XL):
                h = lax.rem(z + nz - dz, nz) * XL + l
                cols = pl.ds(pl.multiple_of(h * HD, HD), HD)
                mixed = jnp.dot(codes[which, :, :, cols].reshape(seqs * tok, HD), had, preferred_element_type=jnp.float32)
                for n in range(seqs):
                    stage[n, h, which] = (mixed[n * tok:(n + 1) * tok] * wide[which, n, :, cols]).astype(jnp.bfloat16)

    dequantize(0)
    pl.semaphore_wait(barrier, len(targets))

    own_kv = pltpu.make_async_copy(stage.at[xh, hc], kv.at[hc, xh, y, c], own_sem.at[0])
    own_kv.start()
    own_q = pltpu.make_async_copy(
        q_hbm.at[xh, :, pl.ds(pl.multiple_of(hc * HD, HD), HD)], qv.at[hc, xh], own_sem.at[1])
    own_q.start()

    def exchange(i, src, dst, send, recv):
        dz, dl, dh = partners[i]
        tz, tl, th = lax.rem(z + nz - dz, nz), xl ^ dl, xh ^ dh
        return pltpu.make_async_remote_copy(
            src_ref=src(tz * XL + tl, th), dst_ref=dst, send_sem=send.at[i], recv_sem=recv.at[i],
            device_id=dev(tz, tl, th, y, c), device_id_type=MESH)

    count = len(partners)
    kv_copies = [exchange(i, lambda h, n: stage.at[n, h], kv.at[hc, xh, y, c], send_kv, recv_kv) for i in range(count)]
    q_copies = [exchange(i, lambda h, n: q_hbm.at[n, :, pl.ds(pl.multiple_of(h * HD, HD), HD)], qv.at[hc, xh],
                         send_q, recv_q) for i in range(count)]
    o_copies = [exchange(i, lambda h, n: ov.at[h, n], out_hbm.at[xh, :, pl.ds(pl.multiple_of(hc * HD, HD), HD)],
                         send_o, recv_o) for i in range(count)]

    def of_plane(copies, k):
        return [cp for p, cp in zip(partners, copies) if p[0] == order[k]]

    def part(k, ya, ca):
        return kv.at[pl.ds(lax.rem(z + order[k], nz) * XL, XL), :, ya, ca]

    def y_copy(k, way, incoming=False):
        ref = part(k, (down if way == 0 else up) if incoming else y, c)
        return pltpu.make_async_remote_copy(
            src_ref=ref, dst_ref=ref, send_sem=send_y.at[way, k], recv_sem=recv_y.at[way, k],
            device_id=dev(z, xl, xh, up if way == 0 else down, c), device_id_type=MESH)

    def relay_copy(k, way, incoming=False):
        ref = kv.at[lax.rem(z + order[k], nz) * XL + way, :, far if incoming else (down if way == 0 else up), c]
        return pltpu.make_async_remote_copy(
            src_ref=ref, dst_ref=ref, send_sem=send_r.at[way, k], recv_sem=recv_r.at[way, k],
            device_id=dev(z, xl, xh, up if way == 0 else down, c), device_id_type=MESH)

    def sib_copy(k, j, ca):
        ref = part(k, (y, down, up, far)[j], ca)
        return pltpu.make_async_remote_copy(
            src_ref=ref, dst_ref=ref, send_sem=send_s.at[j, k], recv_sem=recv_s.at[j, k],
            device_id=dev(z, xl, xh, y, 1 - c), device_id_type=MESH)

    def send_keys(k):
        for cp in of_plane(kv_copies, k):
            cp.start()

    def send_queries():
        for cp in q_copies:
            cp.start()

    def queries():
        for cp in q_copies:
            cp.wait_recv()
        own_q.wait()

    def arrived(k):
        for cp in of_plane(kv_copies, k):
            cp.wait_recv()
        if k == 0:
            own_kv.wait()
        y_copy(k, 0).start()
        y_copy(k, 1).start()
        sib_copy(k, 0, c).start()

    def passed(k):
        for way in range(2):
            y_copy(k, way, True).wait_recv()
            relay_copy(k, way).start()
            sib_copy(k, 1 + way, c).start()

    def rounded(k):
        relay_copy(k, 0, True).wait_recv()
        relay_copy(k, 1, True).wait_recv()
        sib_copy(k, 3, c).start()

    def whole(k):
        for j in range(4):
            sib_copy(k, j, 1 - c).wait_recv()

    for k in range(nz):
        if k:
            dequantize(order[k])
        if k < 3:
            send_keys(k)

    ends = []
    for i in range(doc_ref.shape[1]):
        one = jnp.where(xh == 0, doc_ref[0, i], doc_ref[seqs - 1, i])
        ends.append(one + (ends[-1] if ends else 0))
    lane = lax.broadcasted_iota(jnp.int32, (8, TQ), 1)
    sub = lax.broadcasted_iota(jnp.int32, (8, TQ), 0)

    def prepare(t, _):
        qpos = t * (XL * XH * period) + r * tok + lax.div(lane, tok) * period + lax.rem(lane, tok)
        ds = jnp.zeros((8, TQ), jnp.int32)
        for e in ends:
            ds = jnp.maximum(ds, jnp.where(qpos >= e, e, 0))
        lo_ref[t] = sub - ds + LEAST
        len_ref[t] = qpos - ds + LEAST
        m_ref[t] = jnp.full((8, TQ), NEG, jnp.float32)
        l_ref[t] = jnp.zeros((8, TQ), jnp.float32)
        acc_ref[t] = jnp.zeros((HD, TQ), jnp.float32)
        return 0

    lax.fori_loop(0, nz + 1, prepare, 0)
    for i in range(2):
        mc_ref[i] = jnp.zeros((8, TQ), jnp.float32)
        ratio_ref[i] = jnp.zeros((8, TQ), jnp.float32)
    for ref in (s_a, s_b, p_a, p_b):
        ref[...] = jnp.zeros_like(ref)

    bufs = ((s_a, p_a), (s_b, p_b))
    pieces = CK // SB

    def chunk(zk, h, which, b):
        ys = SB // (CORES * tok)
        return kv[zk * XL + h, b * ys // ny, pl.ds(b * ys % ny, ys), :, which].reshape(SB, HD)

    def scores(t, zk, h):
        s_w = bufs[h][0]
        q = qv[pl.ds(t * XL, XL)].reshape(TQ, HD)
        lo, ln = lo_ref[t] + (zk * XL + h) * CK, len_ref[t]
        old = m_ref[t]
        ms = [old, old]

        def piece(b):
            s = lax.dot_general(chunk(zk, h, 0, b), q, (((1,), (1,)), ((), ())), preferred_element_type=jnp.float32)
            for i in range(SB // 8):
                si = jnp.where(lo + (b * SB + i * 8) <= ln, s[i * 8:(i + 1) * 8], NEG)
                s_w[pl.ds(b * SB + i * 8, 8), :] = si
                ms[i % 2] = jnp.maximum(ms[i % 2], si)

        def finish():
            new = jnp.broadcast_to(jnp.max(jnp.maximum(ms[0], ms[1]), axis=0, keepdims=True), (8, TQ))
            m_ref[t] = new
            mc_ref[h] = new * scale
            ratio_ref[h] = jnp.exp2((old - new) * scale)

        return piece, finish

    def weights(t, h):
        s_r, p_w = bufs[h]
        mc = mc_ref[h]
        ls = [l_ref[t] * ratio_ref[h], jnp.zeros((8, TQ), jnp.float32)]

        def piece(b):
            prev = None
            for i in range(SB // 8):
                p = jnp.exp2(s_r[pl.ds(b * SB + i * 8, 8), :] * scale - mc)
                ls[i % 2] = ls[i % 2] + p
                if i % 2:
                    p_w[pl.ds(b * SB + (i - 1) * 8, 16), :] = jnp.concatenate([prev, p], 0).astype(jnp.bfloat16)
                prev = p

        def finish():
            l_ref[t] = ls[0] + ls[1]

        return piece, finish

    def products(t, zk, h):
        p_r = bufs[h][1]
        acc = [(acc_ref[t].reshape(HD // 8, 8, TQ) * ratio_ref[h][None]).reshape(HD, TQ)]

        def piece(b):
            if b % 2:
                v = jnp.concatenate([chunk(zk, h, 1, b - 1), chunk(zk, h, 1, b)], 0)
                acc[0] = acc[0] + lax.dot_general(
                    v, p_r[pl.ds((b - 1) * SB, 2 * SB), :], (((0,), (0,)), ((), ())), preferred_element_type=jnp.float32)

        def finish():
            acc_ref[t] = acc[0]

        return piece, finish

    def run(parts):
        for b in range(pieces):
            for piece, _ in parts:
                piece(b)
        for _, finish in parts:
            finish()

    def pair_step(t, zk, t_old, zk_old):
        run([products(t_old, zk_old, 0), weights(t_old, 1), scores(t, zk, 0)])
        run([products(t_old, zk_old, 1), weights(t, 0), scores(t, zk, 1)])

    def plane_at(k):
        odd = lax.rem(k, 2)
        return lax.rem(z + odd * lax.div(k + 1, 2) + (1 - odd) * (nz - lax.div(k, 2)), nz)

    todo = {
        (0, 0): [(arrived, 0), (send_queries,), (arrived, 1), (arrived, 2), (send_keys, 3), (send_keys, 4), (passed, 0), (passed, 1),
                 (rounded, 0), (passed, 2), (rounded, 1), (whole, 0), (queries,), (send_keys, 5), (send_keys, 6)],
        (0, 1): [(rounded, 2), (whole, 1)],
        (1, 0): [(arrived, 3), (arrived, 4), (send_keys, 7)],
        (1, 1): [(whole, 2)],
        (2, 0): [(passed, 3)],
        (2, 1): [(passed, 4), (rounded, 3), (arrived, 5)],
        (3, 0): [(arrived, 6), (rounded, 4), (whole, 3)],
        (3, 1): [(passed, 5), (arrived, 7)],
        (4, 0): [(whole, 4), (passed, 6)],
        (4, 1): [(rounded, 5), (passed, 7)],
        (5, 0): [(rounded, 6), (whole, 5)],
        (5, 1): [(rounded, 7)],
        (6, 0): [(whole, 6)],
        (7, 0): [(whole, 7)],
    }

    def with_plane(n, carry):
        zk = plane_at(n)
        tiles = nz // 2 + 1 - (zk - nz // 2 + 1) * lax.div(zk, nz // 2)
        first = lax.div(tiles + 1, 2)

        def with_part(u, carry):
            for (at_n, at_u), steps in todo.items():
                @pl.when(2 * n + u == 2 * at_n + at_u)
                def _(steps=steps):
                    for do, *k in steps:
                        do(*k)

            def with_tile(b, carry):
                t_old, zk_old = carry
                pair_step(zk + b, zk, t_old, zk_old)
                return zk + b, zk

            return lax.fori_loop(u * first, first + u * (tiles - first), with_tile, carry)

        return lax.fori_loop(0, 2, with_part, carry)

    t_old, zk_old = lax.fori_loop(0, nz, with_plane, (jnp.int32(nz), z))
    run([products(t_old, zk_old, 0), weights(t_old, 1)])
    run([products(t_old, zk_old, 1)])

    own_o = pltpu.make_async_copy(
        ov.at[hc, xh], out_hbm.at[xh, :, pl.ds(pl.multiple_of(hc * HD, HD), HD)], own_sem.at[2])
    for k in range(nz)[::-1]:
        t = lax.rem(z + nz - order[k], nz)
        total = jnp.sum(l_ref[t], axis=0, keepdims=True)
        o = (acc_ref[t] / total).T
        ov[pl.ds(t * XL, XL)] = o.astype(jnp.bfloat16).reshape(XL, XH, tok, HD)
        for cp in of_plane(o_copies, k):
            cp.start()
        if k == 0:
            own_o.start()
    own_o.wait()
    for cp in o_copies:
        cp.wait_recv()
    for cp in kv_copies + q_copies + o_copies:
        cp.wait_send()
    for k in range(nz):
        for way in range(2):
            y_copy(k, way).wait_send()
            relay_copy(k, way).wait_send()
        for j in range(4):
            sib_copy(k, j, c).wait_send()


def body(heads, blocks, queries, key_codes, key_scales, value_codes, value_scales, doc_lengths):
    seqs, tok, width = queries.shape
    nz, ny = heads // XL, blocks // (XH * CORES)
    n = heads * XH - 1
    tq, ck = XL * XH * tok, blocks * tok
    dma = pltpu.SemaphoreType.DMA
    vm, hbm = pl.BlockSpec(memory_space=pltpu.VMEM), pl.BlockSpec(memory_space=pl.ANY)
    per_tile = lambda count, dt: pltpu.VMEM((count, 8, tq), dt)
    return pl.pallas_call(
        functools.partial(kernel, heads, blocks),
        out_shape=jax.ShapeDtypeStruct(queries.shape, jnp.bfloat16),
        in_specs=[pl.BlockSpec(memory_space=pltpu.SMEM), hbm, hbm, vm, hbm, vm],
        out_specs=hbm,
        scratch_shapes=[
            pltpu.VMEM((2, seqs, tok, width), jnp.bfloat16),
            pltpu.VMEM((2, seqs, tok, width), jnp.float32),
            pltpu.VMEM((seqs, heads, 2, tok, HD), jnp.bfloat16),
            pltpu.VMEM((heads, XH, ny, CORES, 2, tok, HD), jnp.bfloat16),
            pltpu.VMEM((heads, XH, tok, HD), jnp.bfloat16),
            pltpu.VMEM((heads, XH, tok, HD), jnp.bfloat16),
            pltpu.VMEM((ck, tq), jnp.float32),
            pltpu.VMEM((ck, tq), jnp.float32),
            pltpu.VMEM((ck, tq), jnp.bfloat16),
            pltpu.VMEM((ck, tq), jnp.bfloat16),
            pltpu.VMEM((nz + 1, HD, tq), jnp.float32),
            per_tile(nz + 1, jnp.float32), per_tile(nz + 1, jnp.float32),
            per_tile(nz + 1, jnp.int32), per_tile(nz + 1, jnp.int32),
            per_tile(2, jnp.float32), per_tile(2, jnp.float32),
            dma((n,)), dma((n,)), dma((n,)), dma((n,)), dma((n,)), dma((n,)),
            dma((2, nz)), dma((2, nz)), dma((2, nz)), dma((2, nz)),
            dma((4, nz)), dma((4, nz)), dma((5,)),
        ],
        compiler_params=pltpu.CompilerParams(
            collective_id=0, has_side_effects=True, vmem_limit_bytes=VMEM_ASK),
    )(doc_lengths, queries, key_codes, jnp.transpose(key_scales, (0, 2, 1)),
      value_codes, jnp.transpose(value_scales, (0, 2, 1)))


def solution(mesh):
    rows = P(None, ("head", "blk"), None)
    return jax.shard_map(
        functools.partial(body, mesh.shape["head"], mesh.shape["blk"]),
        mesh=mesh,
        in_specs=(rows, rows, rows, rows, rows, P()),
        out_specs=rows,
        check_vma=False,
    )
```

```python
import functools
import math

import jax
import jax.numpy as jnp
from jax import lax
from jax.experimental import pallas as pl
from jax.experimental.pallas import tpu as pltpu
from jax.sharding import PartitionSpec as P

MESH = pl.DeviceIdType.MESH
NEG = -1e30
LEAST = -(1 << 31)
VMEM_ASK = 60 * 1024 * 1024
HD = 128
XH, XL, CORES = 2, 2, 2


def hadamard_matrix():
    both = lax.broadcasted_iota(jnp.int32, (HD, HD), 0) & lax.broadcasted_iota(jnp.int32, (HD, HD), 1)
    parity = jnp.zeros((HD, HD), jnp.int32)
    for shift in range(7):
        parity = parity + ((both >> shift) & 1)
    return (1 - 2 * (parity & 1)).astype(jnp.float32).astype(jnp.bfloat16)


def kernel(heads, blocks, doc_ref, q_hbm, kc_hbm, ks_ref, vc_hbm, vs_ref, out_hbm,
           codes, wide, stage, kv, qv, ov, s_a, s_b, p_a, p_b, acc_ref, m_ref, l_ref, lo_ref, len_ref, mc_ref, ratio_ref,
           send_kv, send_q, send_o, recv_kv, recv_q, recv_o, send_y, recv_y, send_r, recv_r, send_s, recv_s, own_sem):
    nz, ny = heads // XL, blocks // (XH * CORES)
    half = ny * CORES
    hc, bc = lax.axis_index("head"), lax.axis_index("blk")
    z, xl = lax.div(hc, XL), lax.rem(hc, XL)
    xh, r = lax.div(bc, half), lax.rem(bc, half)
    y, c = lax.div(r, CORES), lax.rem(r, CORES)
    seqs, tok = kc_hbm.shape[0], kc_hbm.shape[1]
    TQ = XL * XH * tok
    CK = XH * half * tok
    SB = 2 * CORES * tok
    period = half * tok
    scale = math.log2(math.e) / math.sqrt(float(HD))

    loads = [pltpu.make_async_copy(ref, codes.at[i], own_sem.at[3 + i]) for i, ref in enumerate((kc_hbm, vc_hbm))]
    for cp in loads:
        cp.start()

    def dev(z_, xl_, xh_, y_, c_):
        return (z_ * XL + xl_, xh_ * half + y_ * CORES + c_)

    up, down, far = lax.rem(y + 1, ny), lax.rem(y + ny - 1, ny), lax.rem(y + 2, ny)
    order = [(k + 1) // 2 if k % 2 else (nz - k // 2) % nz for k in range(nz)]
    offsets = [(dl, dh) for dl in range(XL) for dh in range(XH)]
    partners = [(dz, dl, dh) for dz in order for dl, dh in offsets if (dz, dl, dh) != (0, 0, 0)]
    barrier = pltpu.get_barrier_semaphore()
    targets = [dev(lax.rem(z + dz, nz), xl ^ dl, xh ^ dh, y, c) for dz, dl, dh in partners]
    targets += [dev(z, xl, xh, up, c), dev(z, xl, xh, down, c), dev(z, xl, xh, y, 1 - c)]
    for t in targets:
        pl.semaphore_signal(barrier, inc=1, device_id=t, device_id_type=MESH)

    had = hadamard_matrix()
    head_of_lane = lax.broadcasted_iota(jnp.int32, (heads, heads * HD), 1) // HD
    pick = jnp.where(head_of_lane == lax.broadcasted_iota(jnp.int32, (heads, heads * HD), 0), 1.0, 0.0).astype(jnp.bfloat16)
    for which, scales in enumerate((ks_ref, vs_ref)):
        for n in range(seqs):
            wide[which, n] = lax.dot_general(
                scales[n], pick, (((0,), (0,)), ((), ())), preferred_element_type=jnp.float32) * HD ** (-0.5)
        loads[which].wait()

    def dequantize(dz):
        for which in range(2):
            for l in range(XL):
                h = lax.rem(z + nz - dz, nz) * XL + l
                cols = pl.ds(pl.multiple_of(h * HD, HD), HD)
                mixed = jnp.dot(codes[which, :, :, cols].reshape(seqs * tok, HD), had, preferred_element_type=jnp.float32)
                for n in range(seqs):
                    stage[n, h, which] = (mixed[n * tok:(n + 1) * tok] * wide[which, n, :, cols]).astype(jnp.bfloat16)

    dequantize(0)
    pl.semaphore_wait(barrier, len(targets))

    own_kv = pltpu.make_async_copy(stage.at[xh, hc], kv.at[hc, xh, y, c], own_sem.at[0])
    own_kv.start()
    own_q = pltpu.make_async_copy(
        q_hbm.at[xh, :, pl.ds(pl.multiple_of(hc * HD, HD), HD)], qv.at[hc, xh], own_sem.at[1])
    own_q.start()

    def exchange(i, src, dst, send, recv):
        dz, dl, dh = partners[i]
        tz, tl, th = lax.rem(z + nz - dz, nz), xl ^ dl, xh ^ dh
        return pltpu.make_async_remote_copy(
            src_ref=src(tz * XL + tl, th), dst_ref=dst, send_sem=send.at[i], recv_sem=recv.at[i],
            device_id=dev(tz, tl, th, y, c), device_id_type=MESH)

    count = len(partners)
    kv_copies = [exchange(i, lambda h, n: stage.at[n, h], kv.at[hc, xh, y, c], send_kv, recv_kv) for i in range(count)]
    q_copies = [exchange(i, lambda h, n: q_hbm.at[n, :, pl.ds(pl.multiple_of(h * HD, HD), HD)], qv.at[hc, xh],
                         send_q, recv_q) for i in range(count)]

    def of_plane(copies, k):
        return [cp for p, cp in zip(partners, copies) if p[0] == order[k]]

    def part(k, ya, ca):
        return kv.at[pl.ds(lax.rem(z + order[k], nz) * XL, XL), :, ya, ca]

    def y_copy(k, way, incoming=False):
        ref = part(k, (down if way == 0 else up) if incoming else y, c)
        return pltpu.make_async_remote_copy(
            src_ref=ref, dst_ref=ref, send_sem=send_y.at[way, k], recv_sem=recv_y.at[way, k],
            device_id=dev(z, xl, xh, up if way == 0 else down, c), device_id_type=MESH)

    def relay_copy(k, way, incoming=False):
        ref = kv.at[lax.rem(z + order[k], nz) * XL + way, :, far if incoming else (down if way == 0 else up), c]
        return pltpu.make_async_remote_copy(
            src_ref=ref, dst_ref=ref, send_sem=send_r.at[way, k], recv_sem=recv_r.at[way, k],
            device_id=dev(z, xl, xh, up if way == 0 else down, c), device_id_type=MESH)

    def sib_copy(k, j, ca):
        ref = part(k, (y, down, up, far)[j], ca)
        return pltpu.make_async_remote_copy(
            src_ref=ref, dst_ref=ref, send_sem=send_s.at[j, k], recv_sem=recv_s.at[j, k],
            device_id=dev(z, xl, xh, y, 1 - c), device_id_type=MESH)

    def send_keys(k):
        for cp in of_plane(kv_copies, k):
            cp.start()

    def send_queries():
        for cp in q_copies:
            cp.start()

    def queries():
        for cp in q_copies:
            cp.wait_recv()
        own_q.wait()

    def arrived(k):
        for cp in of_plane(kv_copies, k):
            cp.wait_recv()
        if k == 0:
            own_kv.wait()
        y_copy(k, 0).start()
        y_copy(k, 1).start()
        sib_copy(k, 0, c).start()

    def passed(k):
        for way in range(2):
            y_copy(k, way, True).wait_recv()
            relay_copy(k, way).start()
            sib_copy(k, 1 + way, c).start()

    def rounded(k):
        relay_copy(k, 0, True).wait_recv()
        relay_copy(k, 1, True).wait_recv()
        sib_copy(k, 3, c).start()

    def whole(k):
        for j in range(4):
            sib_copy(k, j, 1 - c).wait_recv()

    for k in range(nz):
        if k:
            dequantize(order[k])
        if k == 3:
            send_queries()
        if k < 5:
            send_keys(k)

    ends = []
    for i in range(doc_ref.shape[1]):
        one = jnp.where(xh == 0, doc_ref[0, i], doc_ref[seqs - 1, i])
        ends.append(one + (ends[-1] if ends else 0))
    lane = lax.broadcasted_iota(jnp.int32, (8, TQ), 1)
    sub = lax.broadcasted_iota(jnp.int32, (8, TQ), 0)

    def prepare(t, _):
        qpos = t * (XL * XH * period) + r * tok + lax.div(lane, tok) * period + lax.rem(lane, tok)
        ds = jnp.zeros((8, TQ), jnp.int32)
        for e in ends:
            ds = jnp.maximum(ds, jnp.where(qpos >= e, e, 0))
        lo_ref[t] = sub - ds + LEAST
        len_ref[t] = qpos - ds + LEAST
        m_ref[t] = jnp.full((8, TQ), NEG, jnp.float32)
        l_ref[t] = jnp.zeros((8, TQ), jnp.float32)
        acc_ref[t] = jnp.zeros((HD, TQ), jnp.float32)
        return 0

    lax.fori_loop(0, nz + 1, prepare, 0)
    for i in range(2):
        mc_ref[i] = jnp.zeros((8, TQ), jnp.float32)
        ratio_ref[i] = jnp.zeros((8, TQ), jnp.float32)
    for ref in (s_a, s_b, p_a, p_b):
        ref[...] = jnp.zeros_like(ref)

    bufs = ((s_a, p_a), (s_b, p_b))
    pieces = CK // SB

    def chunk(zk, h, which, b):
        ys = SB // (CORES * tok)
        return kv[zk * XL + h, b * ys // ny, pl.ds(b * ys % ny, ys), :, which].reshape(SB, HD)

    def scores(t, zk, h):
        s_w = bufs[h][0]
        q = qv[pl.ds(t * XL, XL)].reshape(TQ, HD)
        lo, ln = lo_ref[t] + (zk * XL + h) * CK, len_ref[t]
        old = m_ref[t]
        ms = [old, old]

        def piece(b):
            s = lax.dot_general(chunk(zk, h, 0, b), q, (((1,), (1,)), ((), ())), preferred_element_type=jnp.float32)
            for i in range(SB // 8):
                si = jnp.where(lo + (b * SB + i * 8) <= ln, s[i * 8:(i + 1) * 8], NEG)
                s_w[pl.ds(b * SB + i * 8, 8), :] = si
                ms[i % 2] = jnp.maximum(ms[i % 2], si)

        def finish():
            new = jnp.broadcast_to(jnp.max(jnp.maximum(ms[0], ms[1]), axis=0, keepdims=True), (8, TQ))
            m_ref[t] = new
            mc_ref[h] = new * scale
            ratio_ref[h] = jnp.exp2((old - new) * scale)

        return piece, finish

    def weights(t, h):
        s_r, p_w = bufs[h]
        mc = mc_ref[h]
        ls = [l_ref[t] * ratio_ref[h], jnp.zeros((8, TQ), jnp.float32)]

        def piece(b):
            prev = None
            for i in range(SB // 8):
                p = jnp.exp2(s_r[pl.ds(b * SB + i * 8, 8), :] * scale - mc)
                ls[i % 2] = ls[i % 2] + p
                if i % 2:
                    p_w[pl.ds(b * SB + (i - 1) * 8, 16), :] = jnp.concatenate([prev, p], 0).astype(jnp.bfloat16)
                prev = p

        def finish():
            l_ref[t] = ls[0] + ls[1]

        return piece, finish

    def products(t, zk, h):
        p_r = bufs[h][1]
        acc = [(acc_ref[t].reshape(HD // 8, 8, TQ) * ratio_ref[h][None]).reshape(HD, TQ)]

        def piece(b):
            if b % 2:
                v = jnp.concatenate([chunk(zk, h, 1, b - 1), chunk(zk, h, 1, b)], 0)
                acc[0] = acc[0] + lax.dot_general(
                    v, p_r[pl.ds((b - 1) * SB, 2 * SB), :], (((0,), (0,)), ((), ())), preferred_element_type=jnp.float32)

        def finish():
            acc_ref[t] = acc[0]

        return piece, finish

    def run(parts):
        for b in range(pieces):
            for piece, _ in parts:
                piece(b)
        for _, finish in parts:
            finish()

    def pair_step(t, zk, t_old, zk_old):
        run([products(t_old, zk_old, 0), weights(t_old, 1), scores(t, zk, 0)])
        run([products(t_old, zk_old, 1), weights(t, 0), scores(t, zk, 1)])

    def plane_at(k):
        odd = lax.rem(k, 2)
        return lax.rem(z + odd * lax.div(k + 1, 2) + (1 - odd) * (nz - lax.div(k, 2)), nz)

    todo = {
        (0, 0): [(arrived, 0), (arrived, 1), (arrived, 2), (passed, 0), (passed, 1), (rounded, 0), (passed, 2), (whole, 0), (rounded, 1),
                 (queries,)],
        (0, 1): [(whole, 1), (rounded, 2), (send_keys, 5), (send_keys, 6)],
        (0, 2): [(arrived, 3)],
        (1, 0): [(arrived, 4), (whole, 2), (send_keys, 7)],
        (1, 1): [(passed, 3)],
        (2, 0): [(passed, 4)],
        (2, 1): [(rounded, 3)],
        (2, 2): [(arrived, 5)],
        (3, 0): [(rounded, 4), (whole, 3), (arrived, 6)],
        (3, 1): [(passed, 5)],
        (3, 2): [(arrived, 7)],
        (4, 0): [(whole, 4), (passed, 6)],
        (4, 1): [(rounded, 5)],
        (4, 2): [(passed, 7)],
        (5, 0): [(whole, 5), (rounded, 6)],
        (5, 2): [(rounded, 7)],
        (6, 0): [(whole, 6)],
    }

    def tiles_of(zk):
        return nz // 2 + 1 - (zk - nz // 2 + 1) * lax.div(zk, nz // 2)

    def with_plane(n, carry):
        zk = plane_at(n)
        tiles = tiles_of(zk)

        def with_part(u, carry):
            for (at_n, at_u), steps in todo.items():
                @pl.when(3 * n + u == 3 * at_n + at_u)
                def _(steps=steps):
                    for do, *k in steps:
                        do(*k)

            def with_tile(b, carry):
                t_old, zk_old = carry
                pair_step(zk + b, zk, t_old, zk_old)
                return zk + b, zk

            return lax.fori_loop(lax.div(u * tiles + 2, 3), lax.div((u + 1) * tiles + 2, 3), with_tile, carry)

        return lax.fori_loop(0, 3, with_part, carry)

    t_old, zk_old = lax.fori_loop(0, nz - 1, with_plane, (jnp.int32(nz), z))

    def o_copy(dz, dl, dh, t):
        i = dz * (XL * XH) + dl * XH + dh
        return pltpu.make_async_remote_copy(
            src_ref=ov.at[t * XL + (xl ^ dl), xh ^ dh],
            dst_ref=out_hbm.at[xh, :, pl.ds(pl.multiple_of(hc * HD, HD), HD)],
            send_sem=send_o.at[i], recv_sem=recv_o.at[i],
            device_id=dev(t, xl ^ dl, xh ^ dh, y, c), device_id_type=MESH)

    own_o = pltpu.make_async_copy(
        ov.at[hc, xh], out_hbm.at[xh, :, pl.ds(pl.multiple_of(hc * HD, HD), HD)], own_sem.at[2])

    def close(t):
        total = jnp.sum(l_ref[t], axis=0, keepdims=True)
        o = (acc_ref[t] / total).T
        ov[pl.ds(t * XL, XL)] = o.astype(jnp.bfloat16).reshape(XL, XH, tok, HD)
        dz = lax.rem(z + nz - t, nz)
        for dl, dh in offsets:
            if (dl, dh) == (0, 0):
                @pl.when(t == z)
                def _():
                    own_o.start()

                @pl.when(t != z)
                def _():
                    o_copy(dz, 0, 0, t).start()
            else:
                o_copy(dz, dl, dh, t).start()

    def close_at(t, carry):
        close(t)
        return carry

    whole(nz - 1)
    last = plane_at(nz - 1)
    tiles = tiles_of(last)
    pair_step(last, last, t_old, zk_old)
    lax.fori_loop(0, last, close_at, 0)
    lax.fori_loop(last + tiles, nz, close_at, 0)

    def last_tile(b, carry):
        pair_step(last + b, last, last + b - 1, last)
        close(last + b - 1)
        return carry

    lax.fori_loop(1, tiles, last_tile, 0)
    end = last + tiles - 1
    run([products(end, last, 0), weights(end, 1)])
    run([products(end, last, 1)])
    close(end)
    own_o.wait()
    for dz in range(nz):
        for dl, dh in offsets:
            if (dz, dl, dh) != (0, 0, 0):
                o_copy(dz, dl, dh, lax.rem(z + nz - dz, nz)).wait()
    for cp in kv_copies + q_copies:
        cp.wait_send()
    for k in range(nz):
        for way in range(2):
            y_copy(k, way).wait_send()
            relay_copy(k, way).wait_send()
        for j in range(4):
            sib_copy(k, j, c).wait_send()


def body(heads, blocks, queries, key_codes, key_scales, value_codes, value_scales, doc_lengths):
    seqs, tok, width = queries.shape
    nz, ny = heads // XL, blocks // (XH * CORES)
    n = heads * XH - 1
    tq, ck = XL * XH * tok, blocks * tok
    dma = pltpu.SemaphoreType.DMA
    vm, hbm = pl.BlockSpec(memory_space=pltpu.VMEM), pl.BlockSpec(memory_space=pl.ANY)
    per_tile = lambda count, dt: pltpu.VMEM((count, 8, tq), dt)
    return pl.pallas_call(
        functools.partial(kernel, heads, blocks),
        out_shape=pltpu.VMEM(queries.shape, jnp.bfloat16),
        in_specs=[pl.BlockSpec(memory_space=pltpu.SMEM), hbm, hbm, vm, hbm, vm],
        out_specs=vm,
        scratch_shapes=[
            pltpu.VMEM((2, seqs, tok, width), jnp.bfloat16),
            pltpu.VMEM((2, seqs, tok, width), jnp.float32),
            pltpu.VMEM((seqs, heads, 2, tok, HD), jnp.bfloat16),
            pltpu.VMEM((heads, XH, ny, CORES, 2, tok, HD), jnp.bfloat16),
            pltpu.VMEM((heads, XH, tok, HD), jnp.bfloat16),
            pltpu.VMEM((heads, XH, tok, HD), jnp.bfloat16),
            pltpu.VMEM((ck, tq), jnp.float32),
            pltpu.VMEM((ck, tq), jnp.float32),
            pltpu.VMEM((ck, tq), jnp.bfloat16),
            pltpu.VMEM((ck, tq), jnp.bfloat16),
            pltpu.VMEM((nz + 1, HD, tq), jnp.float32),
            per_tile(nz + 1, jnp.float32), per_tile(nz + 1, jnp.float32),
            per_tile(nz + 1, jnp.int32), per_tile(nz + 1, jnp.int32),
            per_tile(2, jnp.float32), per_tile(2, jnp.float32),
            dma((n,)), dma((n,)), dma((n + 1,)), dma((n,)), dma((n,)), dma((n + 1,)),
            dma((2, nz)), dma((2, nz)), dma((2, nz)), dma((2, nz)),
            dma((4, nz)), dma((4, nz)), dma((5,)),
        ],
        compiler_params=pltpu.CompilerParams(
            collective_id=0, has_side_effects=True, vmem_limit_bytes=VMEM_ASK),
    )(doc_lengths, queries, key_codes, jnp.transpose(key_scales, (0, 2, 1)),
      value_codes, jnp.transpose(value_scales, (0, 2, 1)))


def solution(mesh):
    rows = P(None, ("head", "blk"), None)
    return jax.shard_map(
        functools.partial(body, mesh.shape["head"], mesh.shape["blk"]),
        mesh=mesh,
        in_specs=(rows, rows, rows, rows, rows, P()),
        out_specs=rows,
        check_vma=False,
    )
```

```python
import functools
import math

import jax
import jax.numpy as jnp
from jax import lax
from jax.experimental import pallas as pl
from jax.experimental.pallas import tpu as pltpu
from jax.sharding import PartitionSpec as P

MESH = pl.DeviceIdType.MESH
NEG = -1e30
LEAST = -(1 << 31)
VMEM_ASK = 60 * 1024 * 1024
HD = 128
XH, XL, CORES = 2, 2, 2


def hadamard_matrix():
    both = lax.broadcasted_iota(jnp.int32, (HD, HD), 0) & lax.broadcasted_iota(jnp.int32, (HD, HD), 1)
    parity = jnp.zeros((HD, HD), jnp.int32)
    for shift in range(7):
        parity = parity + ((both >> shift) & 1)
    return (1 - 2 * (parity & 1)).astype(jnp.float32).astype(jnp.bfloat16)


def kernel(heads, blocks, doc_ref, q_hbm, kc_hbm, ks_ref, vc_hbm, vs_ref, out_hbm,
           codes, wide, stage, kv, qv, ov, s_a, s_b, p_a, p_b, acc_ref, m_ref, l_ref, lo_ref, len_ref, mc_ref, ratio_ref,
           send_kv, send_q, send_o, recv_kv, recv_q, recv_o, send_y, recv_y, send_r, recv_r, send_s, recv_s, own_sem):
    nz, ny = heads // XL, blocks // (XH * CORES)
    half = ny * CORES
    hc, bc = lax.axis_index("head"), lax.axis_index("blk")
    z, xl = lax.div(hc, XL), lax.rem(hc, XL)
    xh, r = lax.div(bc, half), lax.rem(bc, half)
    y, c = lax.div(r, CORES), lax.rem(r, CORES)
    seqs, tok = kc_hbm.shape[0], kc_hbm.shape[1]
    TQ = XL * XH * tok
    CK = XH * half * tok
    SB = 2 * CORES * tok
    period = half * tok
    scale = math.log2(math.e) / math.sqrt(float(HD))

    loads = [pltpu.make_async_copy(ref, codes.at[i], own_sem.at[3 + i]) for i, ref in enumerate((kc_hbm, vc_hbm))]
    for cp in loads:
        cp.start()

    def dev(z_, xl_, xh_, y_, c_):
        return (z_ * XL + xl_, xh_ * half + y_ * CORES + c_)

    up, down, far = lax.rem(y + 1, ny), lax.rem(y + ny - 1, ny), lax.rem(y + 2, ny)
    order = [(k + 1) // 2 if k % 2 else (nz - k // 2) % nz for k in range(nz)]
    offsets = [(dl, dh) for dl in range(XL) for dh in range(XH)]
    partners = [(dz, dl, dh) for dz in order for dl, dh in offsets if (dz, dl, dh) != (0, 0, 0)]
    barrier = pltpu.get_barrier_semaphore()
    targets = [dev(lax.rem(z + dz, nz), xl ^ dl, xh ^ dh, y, c) for dz, dl, dh in partners]
    targets += [dev(z, xl, xh, up, c), dev(z, xl, xh, down, c), dev(z, xl, xh, y, 1 - c)]
    for t in targets:
        pl.semaphore_signal(barrier, inc=1, device_id=t, device_id_type=MESH)

    had = hadamard_matrix()
    head_of_lane = lax.broadcasted_iota(jnp.int32, (heads, heads * HD), 1) // HD
    pick = jnp.where(head_of_lane == lax.broadcasted_iota(jnp.int32, (heads, heads * HD), 0), 1.0, 0.0).astype(jnp.bfloat16)
    for which, scales in enumerate((ks_ref, vs_ref)):
        for n in range(seqs):
            wide[which, n] = lax.dot_general(
                scales[n], pick, (((0,), (0,)), ((), ())), preferred_element_type=jnp.float32) * HD ** (-0.5)
        loads[which].wait()

    def dequantize(dz):
        for which in range(2):
            for l in range(XL):
                h = lax.rem(z + nz - dz, nz) * XL + l
                cols = pl.ds(pl.multiple_of(h * HD, HD), HD)
                mixed = jnp.dot(codes[which, :, :, cols].reshape(seqs * tok, HD), had, preferred_element_type=jnp.float32)
                for n in range(seqs):
                    stage[n, h, which] = (mixed[n * tok:(n + 1) * tok] * wide[which, n, :, cols]).astype(jnp.bfloat16)

    dequantize(0)
    pl.semaphore_wait(barrier, len(targets))

    own_kv = pltpu.make_async_copy(stage.at[xh, hc], kv.at[hc, xh, y, c], own_sem.at[0])
    own_kv.start()
    own_q = pltpu.make_async_copy(
        q_hbm.at[xh, :, pl.ds(pl.multiple_of(hc * HD, HD), HD)], qv.at[hc, xh], own_sem.at[1])
    own_q.start()

    def exchange(i, src, dst, send, recv):
        dz, dl, dh = partners[i]
        tz, tl, th = lax.rem(z + nz - dz, nz), xl ^ dl, xh ^ dh
        return pltpu.make_async_remote_copy(
            src_ref=src(tz * XL + tl, th), dst_ref=dst, send_sem=send.at[i], recv_sem=recv.at[i],
            device_id=dev(tz, tl, th, y, c), device_id_type=MESH)

    count = len(partners)
    kv_copies = [exchange(i, lambda h, n: stage.at[n, h], kv.at[hc, xh, y, c], send_kv, recv_kv) for i in range(count)]
    q_copies = [exchange(i, lambda h, n: q_hbm.at[n, :, pl.ds(pl.multiple_of(h * HD, HD), HD)], qv.at[hc, xh],
                         send_q, recv_q) for i in range(count)]

    def of_plane(copies, k):
        return [cp for p, cp in zip(partners, copies) if p[0] == order[k]]

    def part(k, ya, ca):
        return kv.at[pl.ds(lax.rem(z + order[k], nz) * XL, XL), :, ya, ca]

    def y_copy(k, way, incoming=False):
        ref = part(k, (down if way == 0 else up) if incoming else y, c)
        return pltpu.make_async_remote_copy(
            src_ref=ref, dst_ref=ref, send_sem=send_y.at[way, k], recv_sem=recv_y.at[way, k],
            device_id=dev(z, xl, xh, up if way == 0 else down, c), device_id_type=MESH)

    def relay_copy(k, way, incoming=False):
        ref = kv.at[lax.rem(z + order[k], nz) * XL + way, :, far if incoming else (down if way == 0 else up), c]
        return pltpu.make_async_remote_copy(
            src_ref=ref, dst_ref=ref, send_sem=send_r.at[way, k], recv_sem=recv_r.at[way, k],
            device_id=dev(z, xl, xh, up if way == 0 else down, c), device_id_type=MESH)

    def sib_copy(k, j, ca):
        ref = part(k, (y, down, up, far)[j], ca)
        return pltpu.make_async_remote_copy(
            src_ref=ref, dst_ref=ref, send_sem=send_s.at[j, k], recv_sem=recv_s.at[j, k],
            device_id=dev(z, xl, xh, y, 1 - c), device_id_type=MESH)

    def send_keys(k):
        for cp in of_plane(kv_copies, k):
            cp.start()

    def send_queries():
        for cp in q_copies:
            cp.start()

    def queries():
        for cp in q_copies:
            cp.wait_recv()
        own_q.wait()

    def arrived(k):
        for cp in of_plane(kv_copies, k):
            cp.wait_recv()
        if k == 0:
            own_kv.wait()
        sib_copy(k, 0, c).start()
        y_copy(k, 0).start()
        y_copy(k, 1).start()

    def passed(k):
        for way in range(2):
            y_copy(k, way, True).wait_recv()
            sib_copy(k, 1 + way, c).start()
            relay_copy(k, way).start()

    def rounded(k):
        relay_copy(k, 0, True).wait_recv()
        relay_copy(k, 1, True).wait_recv()
        sib_copy(k, 3, c).start()

    def whole(k):
        for j in range(4):
            sib_copy(k, j, 1 - c).wait_recv()

    for k in range(nz):
        if k:
            dequantize(order[k])
        if k == 3:
            send_queries()
        if k < 5:
            send_keys(k)

    ends = []
    for i in range(doc_ref.shape[1]):
        one = jnp.where(xh == 0, doc_ref[0, i], doc_ref[seqs - 1, i])
        ends.append(one + (ends[-1] if ends else 0))
    lane = lax.broadcasted_iota(jnp.int32, (8, TQ), 1)
    sub = lax.broadcasted_iota(jnp.int32, (8, TQ), 0)

    def prepare(t, _):
        qpos = t * (XL * XH * period) + r * tok + lax.div(lane, tok) * period + lax.rem(lane, tok)
        ds = jnp.zeros((8, TQ), jnp.int32)
        for e in ends:
            ds = jnp.maximum(ds, jnp.where(qpos >= e, e, 0))
        lo_ref[t] = sub - ds + LEAST
        len_ref[t] = qpos - ds + LEAST
        m_ref[t] = jnp.full((8, TQ), NEG, jnp.float32)
        l_ref[t] = jnp.zeros((8, TQ), jnp.float32)
        acc_ref[t] = jnp.zeros((HD, TQ), jnp.float32)
        return 0

    lax.fori_loop(0, nz + 1, prepare, 0)
    for i in range(2):
        mc_ref[i] = jnp.zeros((8, TQ), jnp.float32)
        ratio_ref[i] = jnp.zeros((8, TQ), jnp.float32)
    for ref in (s_a, s_b, p_a, p_b):
        ref[...] = jnp.zeros_like(ref)

    bufs = ((s_a, p_a), (s_b, p_b))
    pieces = CK // SB

    def chunk(zk, h, which, b):
        ys = SB // (CORES * tok)
        return kv[zk * XL + h, b * ys // ny, pl.ds(b * ys % ny, ys), :, which].reshape(SB, HD)

    def scores(t, zk, h, own):
        s_w = bufs[h][0]
        q = qv[pl.ds(t * XL, XL)].reshape(TQ, HD)
        lo, ln = lo_ref[t] + (zk * XL + h) * CK, len_ref[t]
        past = lo + LEAST
        old = m_ref[t]
        ms = [old, old]

        def piece(b):
            s = lax.dot_general(chunk(zk, h, 0, b), q, (((1,), (1,)), ((), ())), preferred_element_type=jnp.float32)
            for i in range(SB // 8):
                at = b * SB + i * 8
                seen = lo + at <= ln if own else past >= -at
                si = jnp.where(seen, s[i * 8:(i + 1) * 8], NEG)
                s_w[pl.ds(b * SB + i * 8, 8), :] = si
                ms[i % 2] = jnp.maximum(ms[i % 2], si)

        def finish():
            new = jnp.broadcast_to(jnp.max(jnp.maximum(ms[0], ms[1]), axis=0, keepdims=True), (8, TQ))
            m_ref[t] = new
            mc_ref[h] = new * scale
            ratio_ref[h] = jnp.exp2((old - new) * scale)

        return piece, finish

    def weights(t, h):
        s_r, p_w = bufs[h]
        mc = mc_ref[h]
        ls = [l_ref[t] * ratio_ref[h], jnp.zeros((8, TQ), jnp.float32)]

        def piece(b):
            prev = None
            for i in range(SB // 8):
                p = jnp.exp2(s_r[pl.ds(b * SB + i * 8, 8), :] * scale - mc)
                ls[i % 2] = ls[i % 2] + p
                if i % 2:
                    p_w[pl.ds(b * SB + (i - 1) * 8, 16), :] = jnp.concatenate([prev, p], 0).astype(jnp.bfloat16)
                prev = p

        def finish():
            l_ref[t] = ls[0] + ls[1]

        return piece, finish

    def products(t, zk, h):
        p_r = bufs[h][1]
        acc = [(acc_ref[t].reshape(HD // 8, 8, TQ) * ratio_ref[h][None]).reshape(HD, TQ)]

        def piece(b):
            if b % 2:
                v = jnp.concatenate([chunk(zk, h, 1, b - 1), chunk(zk, h, 1, b)], 0)
                acc[0] = acc[0] + lax.dot_general(
                    v, p_r[pl.ds((b - 1) * SB, 2 * SB), :], (((0,), (0,)), ((), ())), preferred_element_type=jnp.float32)

        def finish():
            acc_ref[t] = acc[0]

        return piece, finish

    def run(parts):
        for b in range(pieces):
            for piece, _ in parts:
                piece(b)
        for _, finish in parts:
            finish()

    def pair_step(own, t, zk, t_old, zk_old):
        run([products(t_old, zk_old, 0), weights(t_old, 1), scores(t, zk, 0, own)])
        run([products(t_old, zk_old, 1), weights(t, 0), scores(t, zk, 1, own)])

    def plane_at(k):
        odd = lax.rem(k, 2)
        return lax.rem(z + odd * lax.div(k + 1, 2) + (1 - odd) * (nz - lax.div(k, 2)), nz)

    todo = {
        (0, 0): [(arrived, 0), (arrived, 1), (arrived, 2), (passed, 0), (passed, 1), (rounded, 0), (passed, 2), (whole, 0), (rounded, 1),
                 (queries,)],
        (0, 1): [(whole, 1), (rounded, 2), (send_keys, 5), (send_keys, 6)],
        (0, 2): [(arrived, 3)],
        (1, 0): [(arrived, 4), (whole, 2), (send_keys, 7)],
        (1, 1): [(passed, 3)],
        (2, 0): [(passed, 4)],
        (2, 1): [(rounded, 3)],
        (2, 2): [(arrived, 5)],
        (3, 0): [(rounded, 4), (whole, 3), (arrived, 6)],
        (3, 1): [(passed, 5)],
        (3, 2): [(arrived, 7)],
        (4, 0): [(whole, 4), (passed, 6)],
        (4, 1): [(rounded, 5)],
        (4, 2): [(passed, 7)],
        (5, 0): [(whole, 5), (rounded, 6)],
        (5, 2): [(rounded, 7)],
        (6, 0): [(whole, 6)],
    }

    def tiles_of(zk):
        return nz // 2 + 1 - (zk - nz // 2 + 1) * lax.div(zk, nz // 2)

    def with_plane(n, carry):
        zk = plane_at(n)
        tiles = tiles_of(zk)

        def with_part(u, carry):
            for (at_n, at_u), steps in todo.items():
                @pl.when(3 * n + u == 3 * at_n + at_u)
                def _(steps=steps):
                    for do, *k in steps:
                        do(*k)

            def with_tile(own, b, carry):
                t_old, zk_old = carry
                pair_step(own, zk + b, zk, t_old, zk_old)
                return zk + b, zk

            low = lax.div(u * tiles + 2, 3)
            high = low + lax.div(2 - u, 2)
            carry = lax.fori_loop(low, high, functools.partial(with_tile, True), carry)
            return lax.fori_loop(high, lax.div((u + 1) * tiles + 2, 3), functools.partial(with_tile, False), carry)

        return lax.fori_loop(0, 3, with_part, carry)

    t_old, zk_old = lax.fori_loop(0, nz - 1, with_plane, (jnp.int32(nz), z))

    def o_copy(dz, dl, dh, t):
        i = dz * (XL * XH) + dl * XH + dh
        return pltpu.make_async_remote_copy(
            src_ref=ov.at[t * XL + (xl ^ dl), xh ^ dh],
            dst_ref=out_hbm.at[xh, :, pl.ds(pl.multiple_of(hc * HD, HD), HD)],
            send_sem=send_o.at[i], recv_sem=recv_o.at[i],
            device_id=dev(t, xl ^ dl, xh ^ dh, y, c), device_id_type=MESH)

    own_o = pltpu.make_async_copy(
        ov.at[hc, xh], out_hbm.at[xh, :, pl.ds(pl.multiple_of(hc * HD, HD), HD)], own_sem.at[2])

    def close(t):
        total = jnp.sum(l_ref[t], axis=0, keepdims=True)
        o = (acc_ref[t] / total).T
        ov[pl.ds(t * XL, XL)] = o.astype(jnp.bfloat16).reshape(XL, XH, tok, HD)
        dz = lax.rem(z + nz - t, nz)
        for dl, dh in offsets:
            if (dl, dh) == (0, 0):
                @pl.when(t == z)
                def _():
                    own_o.start()

                @pl.when(t != z)
                def _():
                    o_copy(dz, 0, 0, t).start()
            else:
                o_copy(dz, dl, dh, t).start()

    def close_at(t, carry):
        close(t)
        return carry

    whole(nz - 1)
    last = plane_at(nz - 1)
    tiles = tiles_of(last)
    pair_step(True, last, last, t_old, zk_old)
    lax.fori_loop(0, last, close_at, 0)
    lax.fori_loop(last + tiles, nz, close_at, 0)

    def last_tile(b, carry):
        pair_step(False, last + b, last, last + b - 1, last)
        close(last + b - 1)
        return carry

    lax.fori_loop(1, tiles, last_tile, 0)
    end = last + tiles - 1
    run([products(end, last, 0), weights(end, 1)])
    run([products(end, last, 1)])
    close(end)
    own_o.wait()
    for dz in range(nz):
        for dl, dh in offsets:
            if (dz, dl, dh) != (0, 0, 0):
                o_copy(dz, dl, dh, lax.rem(z + nz - dz, nz)).wait()
    for cp in kv_copies + q_copies:
        cp.wait_send()
    for k in range(nz):
        for way in range(2):
            y_copy(k, way).wait_send()
            relay_copy(k, way).wait_send()
        for j in range(4):
            sib_copy(k, j, c).wait_send()


def body(heads, blocks, queries, key_codes, key_scales, value_codes, value_scales, doc_lengths):
    seqs, tok, width = queries.shape
    nz, ny = heads // XL, blocks // (XH * CORES)
    n = heads * XH - 1
    tq, ck = XL * XH * tok, blocks * tok
    dma = pltpu.SemaphoreType.DMA
    vm, hbm = pl.BlockSpec(memory_space=pltpu.VMEM), pl.BlockSpec(memory_space=pl.ANY)
    per_tile = lambda count, dt: pltpu.VMEM((count, 8, tq), dt)
    return pl.pallas_call(
        functools.partial(kernel, heads, blocks),
        out_shape=pltpu.VMEM(queries.shape, jnp.bfloat16),
        in_specs=[pl.BlockSpec(memory_space=pltpu.SMEM), hbm, hbm, vm, hbm, vm],
        out_specs=vm,
        scratch_shapes=[
            pltpu.VMEM((2, seqs, tok, width), jnp.bfloat16),
            pltpu.VMEM((2, seqs, tok, width), jnp.float32),
            pltpu.VMEM((seqs, heads, 2, tok, HD), jnp.bfloat16),
            pltpu.VMEM((heads, XH, ny, CORES, 2, tok, HD), jnp.bfloat16),
            pltpu.VMEM((heads, XH, tok, HD), jnp.bfloat16),
            pltpu.VMEM((heads, XH, tok, HD), jnp.bfloat16),
            pltpu.VMEM((ck, tq), jnp.float32),
            pltpu.VMEM((ck, tq), jnp.float32),
            pltpu.VMEM((ck, tq), jnp.bfloat16),
            pltpu.VMEM((ck, tq), jnp.bfloat16),
            pltpu.VMEM((nz + 1, HD, tq), jnp.float32),
            per_tile(nz + 1, jnp.float32), per_tile(nz + 1, jnp.float32),
            per_tile(nz + 1, jnp.int32), per_tile(nz + 1, jnp.int32),
            per_tile(2, jnp.float32), per_tile(2, jnp.float32),
            dma((n,)), dma((n,)), dma((n + 1,)), dma((n,)), dma((n,)), dma((n + 1,)),
            dma((2, nz)), dma((2, nz)), dma((2, nz)), dma((2, nz)),
            dma((4, nz)), dma((4, nz)), dma((5,)),
        ],
        compiler_params=pltpu.CompilerParams(
            collective_id=0, has_side_effects=True, vmem_limit_bytes=VMEM_ASK),
    )(doc_lengths, queries, key_codes, jnp.transpose(key_scales, (0, 2, 1)),
      value_codes, jnp.transpose(value_scales, (0, 2, 1)))


def solution(mesh):
    rows = P(None, ("head", "blk"), None)
    return jax.shard_map(
        functools.partial(body, mesh.shape["head"], mesh.shape["blk"]),
        mesh=mesh,
        in_specs=(rows, rows, rows, rows, rows, P()),
        out_specs=rows,
        check_vma=False,
    )
```
